32 devices in a mesh: wide: 8 (over y, x, core), narrow: 4 (over z).
Axes of the slice: x: 2, y: 2, z: 4, core: 2. Of those that a mesh axis runs over, the one named last changes fastest.
Arguments:
- blocks: float32 [8, 4, 2, 64, 4096], P('wide', 'narrow'), may hold values from -786432 to 786432
- block_coords: int32 [8, 4, 2, 3], P('wide', 'narrow'), may hold values from 0 to 63, as said below
- block_count: int32 [8, 4], P('wide', 'narrow'), may hold values from 0 to 2, as said below
- orbital_factor: float32 [4096, 128], P('narrow'), may hold values from -8 to 8
Outputs:
- aux_new: float32 [4, 4096, 128], P('narrow', 'wide')
- orbital_new: float32 [4096, 128], P('narrow')
The draws below stay inside these ranges and needn't reach their ends.
Inputs may be any that keep to these rules, and one draw needn't show every extreme that they name: `block_coords`: entries are (auxiliary block 0 to 63, orbital block 0 to 63, orbital block 0 to 63); no triple repeats within a column. `block_count`: slot s of a device is live when s < its count; some device holds 2 live blocks in every draw.
All inputs are finite; a program needn't handle non-finite values.
Results may differ from the reference program's by a relative error of at most 0.0003.
Values sent between devices are 32-bit elements; how exact they have to be, the bound alone decides.
No kernel may reach another device: no remote copies, remote signals or barrier semaphores. Data moves between devices by JAX's collectives and lax.ppermute only.
A program may use at most 64 MiB of HBM per device.

```python
import jax
import jax.numpy as jnp
from jax import lax

R = 128
E = 64
NP = 16384
NO = 4096
SLOTS = 2
WIDES = 8
COLS = 4
QB = 64
OB = 64


def draw_block_coords(key, part):
    column_keys = jax.random.split(jax.random.fold_in(key, 11), COLS)

    def one_column(column_key):
        chosen = jax.random.permutation(column_key, QB * OB * OB)[:WIDES * SLOTS]
        aux_block = chosen // (OB * OB)
        first_orb = chosen // OB % OB
        second_orb = chosen % OB
        return jnp.stack([aux_block, first_orb, second_orb], axis=-1).reshape(WIDES, SLOTS, 3)
    columns = jax.vmap(one_column)(column_keys)
    return jnp.transpose(columns, (1, 0, 2, 3)).astype(jnp.int32)


def draw_block_count(key, part):
    count_key, full_key = jax.random.split(jax.random.fold_in(key, 23))
    counts = jax.random.randint(count_key, (WIDES * COLS,), 0, SLOTS + 1)
    full_device = jax.random.randint(full_key, (), 0, WIDES * COLS)
    counts = jnp.where(jnp.arange(WIDES * COLS) == full_device, SLOTS, counts)
    return counts.reshape(WIDES, COLS).astype(jnp.int32)


def draw_orbital_factor(key, part):
    noise_key, mean_key, shape_key = jax.random.split(jax.random.fold_in(key, 37), 3)
    noise = jax.random.normal(noise_key, (NO, R), jnp.float32)
    common = jax.random.normal(mean_key, (NO, 1), jnp.float32)
    profile = jax.random.uniform(shape_key, (1, R), jnp.float32, 0.5, 1.5)
    return jnp.clip(noise + common * profile, -8.0, 8.0).astype(jnp.float32)


def levels(rng, extent, cuts, least, high):
    def one(axis_at, blocks):
        heights = jax.random.uniform(jax.random.fold_in(jax.random.fold_in(rng, 6), axis_at), (blocks,), jnp.float32, least / len(cuts), high / len(cuts))
        return jnp.repeat(jnp.exp(heights), extent[axis_at] // blocks).reshape((-1,) + (1,) * (len(extent) - axis_at - 1))

    level = one(*cuts[0])
    for cut in cuts[1:]:
        level = level * one(*cut)
    return level


def gaussian(own_key, extent, scale, reach, cuts=(), held_as=jnp.bfloat16):
    level = levels(own_key, extent, cuts, -0.22, 0.18) if cuts else 1.0
    result = jax.random.normal(own_key, extent, jnp.float32) * scale * level
    return jnp.minimum(jnp.maximum(result, -reach), reach).astype(held_as)


def setup_inputs(seed: int = 0) -> dict:
    key_of = jax.random.split(jax.random.key(seed), 5)
    blocks = gaussian(key_of[0], (WIDES, COLS, SLOTS, E, E * E), (NO * NO // 128), 786432.0, ((0, 8), (1, 4)), jnp.float32)
    block_coords = draw_block_coords(jax.random.fold_in(key_of[4], 71), 0)
    block_count = draw_block_count(jax.random.fold_in(key_of[4], 71), 0)
    orbital_factor = draw_orbital_factor(jax.random.fold_in(key_of[4], 71), 0)
    return {"blocks": blocks, "block_coords": block_coords, "block_count": block_count, "orbital_factor": orbital_factor}


precise_level = lax.Precision.HIGHEST

def product(left, right):
    return jnp.dot(left.astype(jnp.float32), right.astype(jnp.float32), precision=precise_level, preferred_element_type=jnp.float32)

def inverse_of(gram):
    lower = jnp.linalg.cholesky(gram)
    return jax.scipy.linalg.cho_solve((lower, True), jnp.eye(gram.shape[0], dtype=gram.dtype))

def first_mode(tensor_block, rows_i, rows_j):
    block_edge = rows_i.shape[0]
    contracted = product(tensor_block.reshape(block_edge * block_edge, block_edge), rows_j)
    contracted = contracted.reshape(block_edge, block_edge, -1)
    return (contracted, jnp.sum(contracted * rows_i[None], axis=1))

def second_mode(tensor_block, contracted, aux_rows, rows_i):
    block_edge = rows_i.shape[0]
    term_i = jnp.sum(contracted * aux_rows[:, None, :], axis=0)
    spread = product(aux_rows.T, tensor_block).reshape(-1, block_edge, block_edge)
    term_j = jnp.einsum('rij,ir->jr', spread, rows_i, precision=precise_level)
    return (term_i, term_j)

def pick_rows(matrix, index, length):
    return lax.dynamic_slice_in_dim(matrix, (index * length).astype(jnp.int32), length, 0)

def add_rows(total, start, addend):
    current = lax.dynamic_slice_in_dim(total, start.astype(jnp.int32), addend.shape[0], 0)
    return lax.dynamic_update_slice_in_dim(total, current + addend, start.astype(jnp.int32), 0)

def reference(blocks, block_coords, block_count, orbital_factor):
    wide_count, column_count, slot_count, block_edge = (blocks.shape[0], blocks.shape[1], blocks.shape[2], blocks.shape[3])
    factor_rank = orbital_factor.shape[1]
    column_rows = NP // column_count
    flat_blocks = blocks.reshape(-1, block_edge, block_edge * block_edge)
    flat_coords = block_coords.reshape(-1, 3)
    slot_ids = jnp.arange(slot_count, dtype=jnp.int32)
    weights = (slot_ids[None, None, :] < block_count[:, :, None]).astype(jnp.float32).reshape(-1)
    column_ids = jnp.broadcast_to(jnp.arange(column_count, dtype=jnp.int32)[None, :, None], (wide_count, column_count, slot_count)).reshape(-1)
    gram_b = product(orbital_factor.T, orbital_factor)

    def add_aux(total, item):
        tensor_block, coord, weight, column = item
        rows_i = pick_rows(orbital_factor, coord[1], block_edge)
        rows_j = pick_rows(orbital_factor, coord[2], block_edge)
        unused, aux_term = first_mode(tensor_block, rows_i, rows_j)
        start = column * column_rows + coord[0] * block_edge
        return (add_rows(total, start, weight * aux_term), None)
    aux_sum, unused = lax.scan(add_aux, jnp.zeros((NP, factor_rank), jnp.float32), (flat_blocks, flat_coords, weights, column_ids))
    aux_flat = product(aux_sum, inverse_of(gram_b * gram_b))
    gram_a = product(aux_flat.T, aux_flat)

    def add_orbital(total, item):
        tensor_block, coord, weight, column = item
        rows_i = pick_rows(orbital_factor, coord[1], block_edge)
        rows_j = pick_rows(orbital_factor, coord[2], block_edge)
        contracted, unused = first_mode(tensor_block, rows_i, rows_j)
        start = column * column_rows + coord[0] * block_edge
        aux_rows = lax.dynamic_slice_in_dim(aux_flat, start.astype(jnp.int32), block_edge, 0)
        term_i, term_j = second_mode(tensor_block, contracted, aux_rows, rows_i)
        total = add_rows(total, coord[1] * block_edge, weight * term_i)
        total = add_rows(total, coord[2] * block_edge, weight * term_j)
        return (total, None)
    orbital_sum, unused = lax.scan(add_orbital, jnp.zeros((NO, factor_rank), jnp.float32), (flat_blocks, flat_coords, weights, column_ids))
    orbital_new = product(orbital_sum, inverse_of(2.0 * gram_a * gram_b))
    return (aux_flat.reshape(column_count, column_rows, factor_rank), orbital_new)
```

```python
import jax
import jax.numpy as jnp
from jax import lax
from jax.sharding import PartitionSpec as P

NP = 16384


precise_level = lax.Precision.HIGHEST


def product(left, right):
    return jnp.dot(left, right, precision=precise_level, preferred_element_type=jnp.float32)


def inverse_of(gram):
    lower = jnp.linalg.cholesky(gram)
    return jax.scipy.linalg.cho_solve((lower, True), jnp.eye(gram.shape[0], dtype=gram.dtype))


def digits_of(size):
    digits = []
    stride = 1
    while stride < size:
        left = size // stride
        radix = 2 if left.bit_length() % 2 == 0 else 4
        digits.append((stride, radix))
        stride *= radix
    return digits


def swap_with(value, axis, mask):
    size = lax.axis_size(axis)
    return lax.ppermute(value, axis, [(index, index ^ mask) for index in range(size)])


def gather_from(value, axis):
    size = lax.axis_size(axis)
    held = {0: value}
    for stride, radix in reversed(digits_of(size)):
        fresh = {}
        sent = sorted(held)
        packed = jnp.stack([held[key] for key in sent])
        for digit in range(1, radix):
            arrived = swap_with(packed, axis, digit * stride)
            for place, key in enumerate(sent):
                fresh[key + digit * stride] = arrived[place]
        held.update(fresh)
    return jnp.stack([held[key] for key in range(size)])


def exchange(value, axis):
    size = lax.axis_size(axis)
    for stride, radix in digits_of(size):
        view = value.reshape((size // (stride * radix), radix, stride) + value.shape[1:])
        parts = [view[:, 0]]
        for digit in range(1, radix):
            parts.append(swap_with(view[:, digit], axis, digit * stride))
        value = jnp.stack(parts, axis=1).reshape(value.shape)
    return value


def on_device(blocks, block_coords, block_count, orbital_factor):
    slots = blocks.shape[2]
    edge = blocks.shape[3]
    rank = orbital_factor.shape[1]
    wide_size = lax.axis_size("wide")
    narrow_size = lax.axis_size("narrow")
    wide_at = lax.axis_index("wide")
    narrow_at = lax.axis_index("narrow")
    others = wide_at ^ jnp.arange(wide_size, dtype=jnp.int32)
    columns = narrow_at ^ jnp.arange(narrow_size, dtype=jnp.int32)
    slice_rows = edge // wide_size
    own_blocks = orbital_factor.shape[0] // edge
    column_rows = NP // narrow_size
    own_rows = column_rows // wide_size
    coords = block_coords[0, 0]
    live = (jnp.arange(slots, dtype=jnp.int32) < block_count[0, 0]).astype(jnp.int32)
    tags = jnp.concatenate([coords, live[:, None]], axis=1)

    by_slice = orbital_factor.reshape(own_blocks, wide_size, slice_rows, rank)
    own_slice = lax.dynamic_index_in_dim(by_slice, wide_at, 1, keepdims=False)
    slices = gather_from(own_slice, "narrow").reshape(-1, slice_rows, rank)
    all_tags = gather_from(tags, "wide")
    pair = all_tags[:, :, 1:3].reshape(wide_size, slots * 2)
    place = ((pair // own_blocks) ^ narrow_at) * own_blocks + pair % own_blocks
    wanted = jnp.take(slices, place.reshape(-1), axis=0).reshape(
        wide_size, slots * 2, slice_rows, rank
    )
    pieces = jnp.take(exchange(wanted, "wide"), others, axis=0)
    rows = jnp.transpose(pieces, (1, 0, 2, 3)).reshape(slots, 2, edge, rank)

    gram_b = jnp.sum(gather_from(product(orbital_factor.T, orbital_factor), "narrow"), axis=0)
    inverse_b = inverse_of(gram_b * gram_b)

    terms = []
    for slot in range(slots):
        pairs = (rows[slot, 0][:, None, :] * rows[slot, 1][None, :, :]).reshape(edge * edge, rank)
        terms.append(product(blocks[0, 0, slot], pairs) * live[slot].astype(jnp.float32))
    column_terms = jnp.take(gather_from(jnp.stack(terms), "wide"), others, axis=0)
    column_terms = column_terms.reshape(wide_size * slots, edge, rank)
    column_tags = jnp.take(all_tags, others, axis=0).reshape(wide_size * slots, 4)
    same = column_tags[:, None, 0] == column_tags[None, :, 0]
    order = jnp.arange(wide_size * slots, dtype=jnp.int32)
    first = jnp.argmax(same, axis=1).astype(jnp.int32)
    member = (first[None, :] == order[:, None]).astype(jnp.float32)
    sums = jnp.einsum("st,ter->ser", member, column_terms, precision=precise_level)
    aux = product(sums.reshape(-1, rank), inverse_b)
    gram_a = jnp.sum(gather_from(product(aux.T, aux), "narrow"), axis=0)
    aux = aux.reshape(wide_size * slots, edge, rank)
    target = (
        jnp.arange(own_rows, dtype=jnp.int32) + wide_at * own_rows
    )
    grain = min(own_rows, edge)
    aux_grains = aux.reshape(-1, grain, rank)
    grain_ids = (
        column_tags[:, 0, None] * (edge // grain)
        + jnp.arange(edge // grain, dtype=jnp.int32)[None, :]
    ).reshape(-1)
    wanted_ids = wide_at * (own_rows // grain) + jnp.arange(own_rows // grain, dtype=jnp.int32)
    pick = (wanted_ids[:, None] == grain_ids[None, :]).astype(jnp.float32)
    aux_owned = jnp.einsum("og,ger->oer", pick, aux_grains, precision=precise_level)
    aux_owned = aux_owned.reshape(own_rows, rank)

    orbital_terms = []
    for slot in range(slots):
        mine = jnp.take(first, wide_at * slots + slot)
        aux_rows = jnp.take(aux, mine, axis=0)
        spread = lax.dot_general(
            blocks[0, 0, slot],
            aux_rows,
            (((0,), (0,)), ((), ())),
            precision=precise_level,
            preferred_element_type=jnp.float32,
        ).reshape(edge, edge, rank)
        weight = live[slot].astype(jnp.float32)
        orbital_terms.append(jnp.sum(spread * rows[slot, 1][None], axis=1) * weight)
        orbital_terms.append(jnp.sum(spread * rows[slot, 0][:, None, :], axis=0) * weight)
    by_slice = jnp.stack(orbital_terms).reshape(slots * 2, wide_size, slice_rows, rank)
    outgoing = jnp.transpose(jnp.take(by_slice, others, axis=1), (1, 0, 2, 3))
    arrived = exchange(outgoing, "wide").reshape(wide_size * slots * 2, slice_rows, rank)
    total_blocks = own_blocks * narrow_size
    onehot = (
        jnp.arange(total_blocks, dtype=jnp.int32)[:, None] == pair.reshape(-1)[None, :]
    ).astype(jnp.float32)
    dense = jnp.einsum("bt,ter->ber", onehot, arrived, precision=precise_level)
    dense = dense.reshape(narrow_size, own_blocks, slice_rows, rank)
    owned = jnp.sum(exchange(jnp.take(dense, columns, axis=0), "narrow"), axis=0)
    orbital_sum = jnp.take(gather_from(owned, "wide"), others, axis=0)
    orbital_sum = jnp.transpose(orbital_sum, (1, 0, 2, 3)).reshape(own_blocks * edge, rank)
    orbital_new = product(orbital_sum, inverse_of(2.0 * gram_a * gram_b))
    return (aux_owned[None], orbital_new)


def solution(mesh):
    return jax.shard_map(
        on_device,
        mesh=mesh,
        in_specs=(
            P("wide", "narrow", None, None, None),
            P("wide", "narrow", None, None),
            P("wide", "narrow"),
            P("narrow", None),
        ),
        out_specs=(P("narrow", "wide", None), P("narrow", None)),
        check_vma=False,
    )
```

```python
import functools

import jax
import jax.numpy as jnp
from jax import lax
from jax.experimental import pallas as pl
from jax.experimental.pallas import tpu as pltpu
from jax.sharding import PartitionSpec as P

NP = 16384


precise_level = lax.Precision.HIGHEST
in_vmem = pl.BlockSpec(memory_space=pltpu.VMEM)
in_smem = pl.BlockSpec(memory_space=pltpu.SMEM)


def product(left, right):
    return jnp.dot(left, right, precision=precise_level, preferred_element_type=jnp.float32)


def kernel_call(body, outputs, operands, scalars=0, scratch=(), flops=0):
    moved = sum(int(item.size) * item.dtype.itemsize for item in operands[scalars:])
    moved += sum(int(item.size) * item.dtype.itemsize for item in outputs)
    return pl.pallas_call(
        body,
        out_shape=outputs,
        in_specs=[in_smem] * scalars + [in_vmem] * (len(operands) - scalars),
        out_specs=[in_vmem] * len(outputs),
        scratch_shapes=list(scratch),
        compiler_params=pltpu.CompilerParams(vmem_limit_bytes=48 * 1024 * 1024),
        cost_estimate=pl.CostEstimate(flops=flops, bytes_accessed=moved, transcendentals=0),
    )(*operands)


def shaped(*shape, dtype=jnp.float32):
    return jax.ShapeDtypeStruct(shape, dtype)


def digits_of(size):
    digits = []
    stride = 1
    while stride < size:
        left = size // stride
        radix = 2 if left.bit_length() % 2 == 0 else 4
        digits.append((stride, radix))
        stride *= radix
    return digits


def swap_with(value, axis, mask):
    size = lax.axis_size(axis)
    return lax.ppermute(value, axis, [(index, index ^ mask) for index in range(size)])


def gather_from(value, axis, skip=0):
    digits = digits_of(lax.axis_size(axis))
    held = {0: value}
    for stride, radix in reversed(digits[skip:]):
        fresh = {}
        for digit in range(1, radix):
            for key, item in held.items():
                fresh[key + digit * stride] = swap_with(item, axis, digit * stride)
        held.update(fresh)
    return [held[key] for key in sorted(held)]


def exchange(items, axis, skip=0):
    digits = digits_of(lax.axis_size(axis))
    unit = digits[skip][0] if skip < len(digits) else 1
    items = list(items)
    for stride, radix in digits[skip:]:
        step = stride // unit
        for digit in range(1, radix):
            at = [key for key in range(len(items)) if key // step % radix == digit]
            if len(at) == 1:
                items[at[0]] = swap_with(items[at[0]], axis, digit * stride)
            else:
                packed = swap_with(jnp.stack([items[key] for key in at]), axis, digit * stride)
                for place, key in enumerate(at):
                    items[key] = packed[place]
    return items


def inverse_of(grams, other, scale):
    size = grams[0].shape[0]
    step = 8
    count = size // step
    own = other is None
    operands = list(grams) + ([] if own else [other])
    outputs = [shaped(size, size)] + ([shaped(size, size)] if own else [])

    def body(*refs):
        parts = refs[: len(grams)]
        out_ref = refs[len(operands)]
        sub = lax.broadcasted_iota(jnp.int32, (step, size), 0)
        lane = lax.broadcasted_iota(jnp.int32, (step, size), 1)
        held = []
        for block in range(count):
            at = slice(step * block, step * block + step)
            total = parts[0][at, :]
            for part in parts[1:]:
                total = total + part[at, :]
            if own:
                refs[len(operands) + 1][at, :] = total
                held.append(total * total)
            else:
                held.append(scale * total * refs[len(grams)][at, :])

        def splat_lane(value, index):
            return jnp.broadcast_to(value[:, index : index + 1], (step, size))

        def splat_row(value, index):
            return jnp.broadcast_to(value[index : index + 1, :], (step, size))

        for block in range(count):
            inside = (lane >= step * block) & (lane < step * block + step)
            unit = (lane - step * block == sub).astype(jnp.float32)
            left = [[splat_lane(row, step * block + t) for t in range(step)] for row in held]
            pivots = list(left[block])
            panel = jnp.where(inside, unit, held[block])
            for p in range(step):
                here = sub == p
                inverse = 1.0 / splat_row(pivots[p], p)
                factor = jnp.where(here, -inverse, pivots[p] * inverse)
                for t in range(p + 1, step):
                    pivots[t] = jnp.where(here, 0.0, pivots[t]) - factor * splat_row(pivots[t], p)
                panel = jnp.where(here, 0.0, panel) - factor * splat_row(panel, p)
            rows = [splat_row(panel, t) for t in range(step)]
            fresh = []
            for index in range(count):
                if index == block:
                    fresh.append(panel)
                    continue
                pairs = [left[index][t] * rows[t] for t in range(step)]
                while len(pairs) > 1:
                    pairs = [pairs[t] + pairs[t + 1] for t in range(0, len(pairs), 2)]
                fresh.append(jnp.where(inside, 0.0, held[index]) - pairs[0])
            held = fresh
        for block in range(count):
            out_ref[step * block : step * block + step, :] = held[block]

    return kernel_call(body, outputs, operands, flops=4 * size**3)


def pick_pieces(tags, slices, narrow_at, own_blocks):
    narrow_size, low = len(slices), len(slices[0])
    _, rows, rank = slices[0][0].shape
    slots = tags[0].shape[0]

    def body(at_ref, *refs):
        tag_refs = refs[: len(tags)]
        slice_refs = refs[len(tags) : len(tags) + narrow_size * low]
        out_refs = refs[len(tags) + narrow_size * low :]
        for tag_ref, out_ref in zip(tag_refs, out_refs):
            for pair in range(slots * 2):
                block = tag_ref[pair // 2, 1 + pair % 2]
                owner = (block // own_blocks) ^ at_ref[0]
                local = block % own_blocks
                for j in range(low):
                    value = slice_refs[j][local]
                    for m in range(1, narrow_size):
                        value = jnp.where(owner == m, slice_refs[m * low + j][local], value)
                    out_ref[pair, j] = value

    return kernel_call(
        body,
        [shaped(slots * 2, low, rows, rank)] * len(tags),
        [narrow_at] + list(tags) + [item for group in slices for item in group],
        scalars=1 + len(tags),
    )


def lay_rows(wide_at, pieces, wide_size):
    pairs, low, rows, rank = pieces[0].shape

    def body(at_ref, *refs):
        out_ref = refs[-1]
        for d, piece_ref in enumerate(refs[:-1]):
            for j in range(low):
                place = at_ref[0] ^ (d * low + j)
                for pair in range(pairs):
                    out_ref[pair, place] = piece_ref[pair, j]

    return kernel_call(
        body, [shaped(pairs, wide_size, rows, rank)], [wide_at] + list(pieces), scalars=1
    )[0]


def split_blocks(blocks):
    slots, edge, pairs = blocks.shape
    chunk = min(pairs, 512)

    def body(in_ref, out_ref):
        value = in_ref[0]
        high = value.astype(jnp.bfloat16).astype(jnp.float32)
        rest = value - high
        middle = rest.astype(jnp.bfloat16).astype(jnp.float32)
        low = rest - middle
        stacked = jnp.concatenate([high, middle, low, high], axis=0)
        out_ref[0] = stacked.T.astype(jnp.bfloat16)

    return pl.pallas_call(
        body,
        out_shape=shaped(slots, pairs, 4 * edge, dtype=jnp.bfloat16),
        grid=(slots, pairs // chunk),
        in_specs=[pl.BlockSpec((1, edge, chunk), lambda s, c: (s, 0, c))],
        out_specs=pl.BlockSpec((1, chunk, 4 * edge), lambda s, c: (s, c, 0)),
        compiler_params=pltpu.CompilerParams(vmem_limit_bytes=48 * 1024 * 1024),
        cost_estimate=pl.CostEstimate(
            flops=0, bytes_accessed=slots * edge * pairs * 12, transcendentals=0
        ),
    )(blocks)


def split3(value):
    high = value.astype(jnp.bfloat16)
    rest = value - high.astype(jnp.float32)
    middle = rest.astype(jnp.bfloat16)
    low = (rest - middle.astype(jnp.float32)).astype(jnp.bfloat16)
    return high, middle, low


def second_mode(wide_at, tags, terms, inverse, spread_blocks, rows, wide_size, low):
    slots, edge, rank = terms[0].shape
    pairs = spread_blocks.shape[1]
    slice_rows = edge // wide_size
    chunk = 4

    def body(at_ref, tag_ref, *refs):
        term_refs = refs[: len(terms)]
        inverse_ref, spread_ref, rows_ref = refs[len(terms) : len(terms) + 3]
        out_refs = refs[len(terms) + 3 : len(terms) + 3 + low]
        held_ref = refs[-1]
        sums = []
        for slot in range(slots):
            total = None
            for m, term_ref in enumerate(term_refs):
                for other in range(slots):
                    same = (tag_ref[m, other, 0] == tag_ref[0, slot, 0]).astype(jnp.float32)
                    part = term_ref[other] * same
                    total = part if total is None else total + part
            sums.append(total)
        aux = product(jnp.concatenate(sums, axis=0), inverse_ref[...])
        for slot in range(slots):
            weight = tag_ref[0, slot, 3].astype(jnp.float32)
            high, middle, least = split3(aux[slot * edge : (slot + 1) * edge] * weight)
            none = jnp.zeros_like(high)
            stacked = jnp.concatenate(
                [
                    jnp.concatenate([high, high, high, none], axis=0),
                    jnp.concatenate([middle, middle, none, least], axis=0),
                ],
                axis=1,
            )
            rows_i, rows_j = rows_ref[2 * slot], rows_ref[2 * slot + 1]

            def step(index, total_j):
                at = pl.multiple_of(index * (chunk * edge), chunk * edge)
                spread = jnp.dot(
                    spread_ref[slot, pl.ds(at, chunk * edge), :],
                    stacked,
                    preferred_element_type=jnp.float32,
                )
                spread = spread[:, :rank] + spread[:, rank:]
                for inner in range(chunk):
                    part = spread[inner * edge : (inner + 1) * edge]
                    here = index * chunk + inner
                    held_ref[2 * slot, pl.ds(here, 1), :] = jnp.sum(
                        part * rows_j, axis=0, keepdims=True
                    )
                    total_j = total_j + part * rows_ref[2 * slot, pl.ds(here, 1), :]
                return total_j

            held_ref[2 * slot + 1] = lax.fori_loop(
                0, edge // chunk, step, jnp.zeros((edge, rank), jnp.float32), unroll=True
            )
        for place in range(wide_size):
            source = (at_ref[0] ^ place) * slice_rows
            for pair in range(2 * slots):
                out_refs[place % low][place // low, pair] = held_ref[
                    pair, pl.ds(pl.multiple_of(source, slice_rows), slice_rows), :
                ]

    return kernel_call(
        body,
        [shaped(wide_size // low, 2 * slots, slice_rows, rank)] * low,
        [wide_at, tags] + list(terms) + [inverse, spread_blocks, rows],
        scalars=2,
        scratch=[pltpu.VMEM((2 * slots, edge, rank), jnp.float32)],
        flops=slots * 2 * pairs * 4 * edge * 2 * rank,
    )


def column_rows(wide_at, tags, first, terms, inverse, own_rows):
    slots, edge, rank = terms[0].shape
    count = slots * len(terms)
    grain = min(own_rows, edge)

    def body(at_ref, tag_ref, first_ref, *refs):
        term_refs = refs[: len(terms)]
        inverse_ref, gram_ref, out_ref, held_ref = refs[len(terms) :]
        held_ref[...] = jnp.zeros_like(held_ref)
        for index in range(count):
            to = first_ref[index]
            held_ref[to] += term_refs[index // slots][index % slots]
        aux = product(held_ref[...].reshape(count * edge, rank), inverse_ref[...])
        held_ref[...] = aux.reshape(count, edge, rank)
        gram_ref[...] = lax.dot_general(
            aux,
            aux,
            (((0,), (0,)), ((), ())),
            precision=precise_level,
            preferred_element_type=jnp.float32,
        )
        out_ref[...] = jnp.zeros_like(out_ref)
        per_block = edge // grain
        per_device = own_rows // grain
        for index in range(count):
            for part in range(per_block):
                grain_at = tag_ref[index // slots, index % slots, 0] * per_block + part

                @pl.when((first_ref[index] == index) & (grain_at // per_device == at_ref[0]))
                def _():
                    out_ref[grain_at % per_device] = held_ref[
                        index, part * grain : (part + 1) * grain, :
                    ]

    gram, owned = kernel_call(
        body,
        [shaped(rank, rank), shaped(own_rows // grain, grain, rank)],
        [wide_at, tags, first] + list(terms) + [inverse],
        scalars=3,
        scratch=[pltpu.VMEM((count, edge, rank), jnp.float32)],
        flops=4 * count * edge * rank * rank,
    )
    return gram, owned.reshape(own_rows, rank)


def pack_pieces(groups):
    low = len(groups)
    partners = groups[0].shape[0]

    def body(*refs):
        for d in range(partners):
            for j in range(low):
                refs[low + d][j] = refs[j][d]

    return kernel_call(body, [shaped(low, *groups[0].shape[1:])] * partners, list(groups))


def add_pieces(narrow_at, tags, pieces, narrow_size, own_blocks):
    low, pairs, rows, rank = pieces[0].shape

    def body(at_ref, tag_ref, *refs):
        piece_refs = refs[: len(pieces)]
        out_refs = refs[len(pieces) : len(pieces) + narrow_size]
        held_ref = refs[-1]
        held_ref[...] = jnp.zeros_like(held_ref)
        for d, piece_ref in enumerate(piece_refs):
            for j in range(low):
                for pair in range(pairs):
                    block = tag_ref[d * low + j, pair // 2, 1 + pair % 2]
                    held_ref[block] += piece_ref[j, pair]
        for m, out_ref in enumerate(out_refs):
            owner = at_ref[0] ^ m
            out_ref[...] = held_ref[pl.ds(owner * own_blocks, own_blocks)]

    return kernel_call(
        body,
        [shaped(own_blocks, rows, rank)] * narrow_size,
        [narrow_at, tags] + list(pieces),
        scalars=2,
        scratch=[pltpu.VMEM((narrow_size * own_blocks, rows, rank), jnp.float32)],
    )


def solve_rows(parts, inverse):
    own_blocks, rows, rank = parts[0].shape

    def body(*refs):
        total = refs[0][...]
        for ref in refs[1 : len(parts)]:
            total = total + ref[...]
        solved = product(total.reshape(own_blocks * rows, rank), refs[len(parts)][...])
        refs[-1][...] = solved.reshape(own_blocks, rows, rank)

    return kernel_call(
        body,
        [shaped(own_blocks, rows, rank)],
        list(parts) + [inverse],
        flops=2 * own_blocks * rows * rank * rank,
    )[0]


def lay_result(wide_at, parts):
    own_blocks, rows, rank = parts[0].shape

    def body(at_ref, *refs):
        for m, ref in enumerate(refs[:-1]):
            place = at_ref[0] ^ m
            for block in range(own_blocks):
                refs[-1][block, place] = ref[block]

    return kernel_call(
        body,
        [shaped(own_blocks, len(parts), rows, rank)],
        [wide_at] + list(parts),
        scalars=1,
    )[0]


def on_device(blocks, block_coords, block_count, orbital_factor):
    slots, edge = blocks.shape[2:4]
    rank = orbital_factor.shape[1]
    wide_size = lax.axis_size("wide")
    narrow_size = lax.axis_size("narrow")
    low = digits_of(wide_size)[0][1]
    wide_index = lax.axis_index("wide")
    wide_at = wide_index.reshape(1)
    narrow_at = lax.axis_index("narrow").reshape(1)
    slice_rows = edge // wide_size
    own_blocks = orbital_factor.shape[0] // edge
    own_rows = NP // narrow_size // wide_size
    live = (jnp.arange(slots, dtype=jnp.int32) < block_count[0, 0]).astype(jnp.int32)
    tags = jnp.concatenate([block_coords[0, 0], live[:, None]], axis=1)

    by_slice = orbital_factor.reshape(own_blocks, wide_size, slice_rows, rank)
    own_slices = [
        lax.dynamic_index_in_dim(by_slice, wide_index ^ j, 1, keepdims=False) for j in range(low)
    ]
    slices = [[item] for item in gather_from(own_slices[0], "narrow")]
    slices[0] = own_slices
    for group in slices[1:]:
        group.extend(swap_with(group[0], "wide", j) for j in range(1, low))
    partner_tags = gather_from(tags, "wide", skip=1)
    wanted = pick_pieces(partner_tags, slices, narrow_at, own_blocks)
    rows = lay_rows(wide_at, exchange(wanted, "wide", skip=1), wide_size)
    rows = rows.reshape(slots * 2, edge, rank)
    near = jnp.stack(partner_tags)
    all_tags = jnp.stack([near] + [swap_with(near, "wide", j) for j in range(1, low)], axis=1)
    all_tags = all_tags.reshape(wide_size, slots, 4)

    grams = gather_from(product(orbital_factor.T, orbital_factor), "narrow")
    inverse_b, gram_b = inverse_of(grams, None, 1.0)

    spread_blocks = split_blocks(blocks[0, 0])
    terms = []
    for slot in range(slots):
        pairs = rows[2 * slot][:, None, :] * rows[2 * slot + 1][None, :, :]
        term = product(blocks[0, 0, slot], pairs.reshape(edge * edge, rank))
        terms.append(term * live[slot].astype(jnp.float32))
    column_terms = gather_from(jnp.stack(terms), "wide")

    groups = second_mode(
        wide_at, all_tags, column_terms, inverse_b, spread_blocks, rows, wide_size, low
    )

    blocks_at = all_tags[:, :, 0].reshape(-1)
    first = jnp.argmax(blocks_at[:, None] == blocks_at[None, :], axis=1).astype(jnp.int32)
    gram_part, aux_owned = column_rows(
        wide_at, all_tags, first, column_terms, inverse_b, own_rows
    )
    inverse_a, = inverse_of(gather_from(gram_part, "narrow"), gram_b, 2.0)

    groups = [groups[0]] + [swap_with(groups[j], "wide", j) for j in range(1, low)]
    pieces = exchange(pack_pieces(groups), "wide", skip=1)
    sums = add_pieces(narrow_at, all_tags, pieces, narrow_size, own_blocks)
    solved = solve_rows(exchange(sums, "narrow"), inverse_a)
    orbital_new = lay_result(wide_at, gather_from(solved, "wide"))
    return (aux_owned[None], orbital_new.reshape(own_blocks * edge, rank))


def solution(mesh):
    return jax.shard_map(
        on_device,
        mesh=mesh,
        in_specs=(
            P("wide", "narrow", None, None, None),
            P("wide", "narrow", None, None),
            P("wide", "narrow"),
            P("narrow", None),
        ),
        out_specs=(P("narrow", "wide", None), P("narrow", None)),
        check_vma=False,
    )
```

```python
import functools

import jax
import jax.numpy as jnp
from jax import lax
from jax.experimental import pallas as pl
from jax.experimental.pallas import tpu as pltpu
from jax.sharding import PartitionSpec as P

NP = 16384


precise_level = lax.Precision.HIGHEST
in_vmem = pl.BlockSpec(memory_space=pltpu.VMEM)
in_smem = pl.BlockSpec(memory_space=pltpu.SMEM)
live_at = 3
in_hbm = pl.BlockSpec(memory_space=pltpu.HBM)


def product(left, right):
    return jnp.dot(left, right, precision=precise_level, preferred_element_type=jnp.float32)


def kernel_call(body, outputs, operands, scalars=0, scratch=(), about_us=0.3, after=(), far=False):
    after = list(after)

    def whole(*refs):
        body(*refs[: len(operands)], *refs[len(operands) + len(after) :])

    return pl.pallas_call(
        whole,
        out_shape=outputs,
        in_specs=[in_smem] * scalars
        + [in_hbm if far else in_vmem] * (len(operands) - scalars)
        + [pl.BlockSpec(memory_space=pl.ANY)] * len(after),
        out_specs=[in_vmem] * len(outputs),
        scratch_shapes=list(scratch),
        compiler_params=pltpu.CompilerParams(vmem_limit_bytes=24 * 1024 * 1024),
        cost_estimate=pl.CostEstimate(
            flops=int(about_us * 1e6), bytes_accessed=0, transcendentals=0
        ),
    )(*operands, *after)


def shaped(*shape, dtype=jnp.float32):
    return jax.ShapeDtypeStruct(shape, dtype)


def add_tree(items):
    while len(items) > 1:
        items = [items[t] + items[t + 1] for t in range(0, len(items), 2)]
    return items[0]


def digits_of(size):
    digits = []
    stride = 1
    while stride < size:
        left = size // stride
        radix = 2 if left.bit_length() % 2 == 0 else 4
        digits.append((stride, radix))
        stride *= radix
    return digits


def swap_with(value, axis, mask):
    size = lax.axis_size(axis)
    return lax.ppermute(value, axis, [(index, index ^ mask) for index in range(size)])


def send_by_core(value, masks):
    wide_size, narrow_size = lax.axis_size("wide"), lax.axis_size("narrow")
    pairs = [
        (w * narrow_size + n, w * narrow_size + (n ^ masks[w % len(masks)]))
        for w in range(wide_size)
        for n in range(narrow_size)
    ]
    return lax.ppermute(value, ("wide", "narrow"), pairs)


def gather_from(value, axis, skip=0):
    digits = digits_of(lax.axis_size(axis))
    held = {0: value}
    for stride, radix in reversed(digits[skip:]):
        fresh = {}
        for digit in range(1, radix):
            for key, item in held.items():
                fresh[key + digit * stride] = swap_with(item, axis, digit * stride)
        held.update(fresh)
    return [held[key] for key in sorted(held)]


def exchange(items, axis, skip=0):
    digits = digits_of(lax.axis_size(axis))
    unit = digits[skip][0] if skip < len(digits) else 1
    items = list(items)
    for stride, radix in digits[skip:]:
        step = stride // unit
        for digit in range(1, radix):
            at = [key for key in range(len(items)) if key // step % radix == digit]
            if len(at) == 1:
                items[at[0]] = swap_with(items[at[0]], axis, digit * stride)
            else:
                packed = swap_with(jnp.stack([items[key] for key in at]), axis, digit * stride)
                for place, key in enumerate(at):
                    items[key] = packed[place]
    return items


def inverse_of(grams, other, scale, after=()):
    size = grams[0].shape[-1]
    step = 16
    count = size // step
    own = other is None
    operands = list(grams) + ([] if own else [other])
    outputs = [shaped(size, size)] + ([shaped(size, size)] if own else [])

    def body(*refs):
        parts = refs[: len(grams)]
        out_ref = refs[len(operands)]
        left_ref, right_ref = refs[-2:]
        sub = lax.broadcasted_iota(jnp.int32, (step, size), 0)
        lane = lax.broadcasted_iota(jnp.int32, (step, size), 1)
        held = []
        for block in range(count):
            at = slice(step * block, step * block + step)
            total = add_tree([part[pl.ds(part.shape[0] - size + step * block, step), :] for part in parts])
            if own:
                refs[len(operands) + 1][at, :] = total
                held.append(total * total)
            else:
                held.append(scale * total * refs[len(grams)][at, :])

        def splat_lane(value, index):
            return jnp.broadcast_to(value[:, index : index + 1], (step, size))

        def splat_row(value, index):
            return jnp.broadcast_to(value[index : index + 1, :], (step, size))

        for block in range(count):
            at = slice(step * block, step * block + step)
            inside = (lane >= step * block) & (lane < step * block + step)
            upto = lane < step * block + step
            unit = (lane - step * block == sub).astype(jnp.float32)
            pivots = [splat_lane(held[block], step * block + t) for t in range(step)]
            panel = jnp.where(inside, unit, held[block])
            left_ref[at, :] = jnp.where(upto, panel, 0.0)
            for p in range(0, step, 2):
                first, second = sub == p, sub == p + 1
                corner = splat_row(pivots[p], p)
                above, below = splat_row(pivots[p + 1], p), splat_row(pivots[p], p + 1)
                last = splat_row(pivots[p + 1], p + 1)
                scaled = 1.0 / (corner * last - above * below)
                i11, i12, i21, i22 = last * scaled, -above * scaled, -below * scaled, corner * scaled
                one = jnp.where(
                    first, -i11, jnp.where(second, -i21, pivots[p] * i11 + pivots[p + 1] * i21)
                )
                two = jnp.where(
                    first, -i12, jnp.where(second, -i22, pivots[p] * i12 + pivots[p + 1] * i22)
                )

                def clear(value):
                    kept = jnp.where(first | second, 0.0, value)
                    return kept - (one * splat_row(value, p) + two * splat_row(value, p + 1))

                for t in range(p + 2, step):
                    pivots[t] = clear(pivots[t])
                panel = clear(panel)
            right_ref[at, :] = jnp.where(upto, panel, 0.0)
            rows = [splat_row(panel, t) for t in range(step)]
            for index in range(block + 1, count):
                pairs = [splat_lane(held[index], step * block + t) * rows[t] for t in range(step)]
                held[index] = jnp.where(inside, 0.0, held[index]) - add_tree(pairs)
        out_ref[...] = lax.dot_general(
            left_ref[...],
            right_ref[...],
            (((0,), (0,)), ((), ())),
            precision=precise_level,
            preferred_element_type=jnp.float32,
        )

    return kernel_call(
        body,
        outputs,
        operands,
        scratch=[pltpu.VMEM((size, size), jnp.float32)] * 2,
        about_us=3.5,
        after=after,
    )


def own_part(chip_slice):
    own_blocks, low, rows, rank = chip_slice.shape

    def body(in_ref, out_ref):
        core = lax.axis_index("wide") % low
        for block in range(own_blocks):
            out_ref[block] = in_ref[block, core]

    return kernel_call(body, [shaped(own_blocks, rows, rank)], [chip_slice])[0]


def open_tags(coords, count, after):
    slots, axes = coords.shape
    rank = after[0].shape[-1]

    def body(coords_ref, count_ref, tag_ref, out_ref):
        slot_at = lax.broadcasted_iota(jnp.int32, (slots, 1), 0)
        tag_ref[...] = jnp.zeros_like(tag_ref)
        tag_ref[:slots, :axes] = coords_ref[...].astype(jnp.float32)
        tag_ref[:slots, axes : axes + 1] = (slot_at < count_ref[...]).astype(jnp.float32)
        out_ref[...] = coords_ref[...]

    return kernel_call(
        body,
        [shaped(8, rank), shaped(slots, axes, dtype=jnp.int32)],
        [coords, count],
        after=after,
    )


def stage(value, after):
    def body(in_ref, out_ref, sem):
        copy = pltpu.make_async_copy(in_ref, out_ref, sem)
        copy.start()
        copy.wait()

    return kernel_call(
        body,
        [shaped(*value.shape)],
        [value],
        scratch=[pltpu.SemaphoreType.DMA],
        after=after,
        far=True,
    )[0]


def pack_slices(pairs, single, after):
    own_blocks, low, rows, rank = pairs[0].shape if pairs else (single.shape[0], 0, 0, 0)
    _, rows, rank = single.shape
    total = own_blocks * (low * len(pairs) + 1)

    def body(*refs):
        out_ref = refs[-1]
        for index, ref in enumerate(refs[: len(pairs)]):
            at = index * own_blocks * low
            out_ref[at : at + own_blocks * low] = ref[...].reshape(own_blocks * low, rows, rank)
        out_ref[total - own_blocks :] = refs[len(pairs)][...]

    return kernel_call(
        body, [shaped(total, rows, rank)], list(pairs) + [single], after=after
    )[0]


def pick_pieces(coords, own, mine, theirs, narrow_size, after):
    own_blocks, low, rows, rank = own.shape
    partners, slots, _ = coords.shape
    piece_rows = slots * 2 * low * rows

    def body(coord_ref, own_ref, mine_ref, theirs_ref, *out_refs):
        narrow_at = lax.axis_index("narrow")
        core = lax.axis_index("wide") % low
        for d, out_ref in enumerate(out_refs):
            for pair in range(slots * 2):
                block = coord_ref[d, pair // 2, 1 + pair % 2]
                owner = (block // own_blocks) ^ narrow_at
                local = block % own_blocks
                before = jnp.maximum(owner, 1) - 1
                last = before == narrow_size - 2
                for j in range(low):
                    slice_at = core ^ j
                    holder = jnp.where(last, slice_at, before % low)
                    at = jnp.where(
                        last,
                        (narrow_size - 2) * own_blocks + local,
                        (before // low * own_blocks + local) * low + slice_at,
                    )
                    away = jnp.where(holder == core, mine_ref[at], theirs_ref[at])
                    to = (pair * low + j) * rows
                    out_ref[to : to + rows, :] = jnp.where(
                        owner == 0, own_ref[local, slice_at], away
                    )
        here, there = mine_ref[...].reshape(-1, rank), theirs_ref[...].reshape(-1, rank)
        rows_of = [jnp.where(core == j, here, there) for j in range(low)]
        gram = join_gram(
            gram_parts(jnp.concatenate([own_ref[...].reshape(-1, rank)] + rows_of, axis=0))
        )
        for out_ref in out_refs:
            out_ref[piece_rows:, :] = gram

    return kernel_call(
        body,
        [shaped(piece_rows + rank, rank)] * partners,
        [coords, own, mine, theirs],
        scalars=1,
        after=after,
    )


def first_mode(tags, pieces, blocks, wide_size, low, after):
    rank = pieces[0].shape[1]
    slots, edge, _ = blocks.shape
    pairs = 2 * slots
    slice_rows = edge // wide_size
    chunk = max(1, 256 // edge)

    def body(tag_ref, *refs):
        piece_refs = refs[: len(pieces)]
        blocks_ref, rows_ref, term_ref, held_ref = refs[len(pieces) :]
        term_ref[slots * edge :, :] = tag_ref[...]
        wide_at = lax.axis_index("wide")
        for d, piece_ref in enumerate(piece_refs):
            for j in range(low):
                place = wide_at ^ (d * low + j)
                for pair in range(pairs):
                    at = (pair * low + j) * slice_rows
                    held_ref[pair, place] = piece_ref[at : at + slice_rows, :]
        rows_ref[...] = held_ref[...].reshape(pairs, edge, rank)
        for slot in range(slots):
            rows_j = rows_ref[2 * slot + 1]

            def step(index, totals):
                wide_total, thin_total = totals
                products = jnp.concatenate(
                    [
                        rows_ref[2 * slot, pl.ds(index * chunk + inner, 1), :] * rows_j
                        for inner in range(chunk)
                    ],
                    axis=0,
                )
                high, middle, least = split3(products)
                at = pl.ds(pl.multiple_of(index * (chunk * edge), chunk * edge), chunk * edge)
                left = jnp.concatenate(split3(blocks_ref[slot, :, at]), axis=0)
                wide_total = wide_total + jnp.dot(
                    left,
                    jnp.concatenate([high, middle], axis=1),
                    preferred_element_type=jnp.float32,
                )
                thin_total = thin_total + jnp.dot(
                    left[:edge], least, preferred_element_type=jnp.float32
                )
                return wide_total, thin_total

            wide_total, thin_total = lax.fori_loop(
                0,
                edge // chunk,
                step,
                (
                    jnp.zeros((3 * edge, 2 * rank), jnp.float32),
                    jnp.zeros((edge, rank), jnp.float32),
                ),
                unroll=True,
            )
            total = wide_total[:, :rank] + wide_total[:, rank:]
            total = thin_total + total[2 * edge :] + total[edge : 2 * edge] + total[:edge]
            live = tag_ref[slot : slot + 1, live_at : live_at + 1]
            term_ref[slot * edge : (slot + 1) * edge, :] = total * live

    return kernel_call(
        body,
        [shaped(pairs, edge, rank), shaped(slots * edge + tags.shape[0], rank)],
        [tags] + list(pieces) + [blocks],
        scratch=[pltpu.VMEM((pairs, wide_size, slice_rows, rank), jnp.float32)],
        about_us=3.0,
        after=after,
    )


def turn_blocks(blocks, after):
    slots, edge, pairs = blocks.shape
    chunk = min(pairs, 512)

    def body(in_ref, turned_ref):
        for slot in range(slots):

            @pl.loop(0, pairs // chunk)
            def _(index):
                at = pl.ds(pl.multiple_of(index * chunk, chunk), chunk)
                high, middle, low = split3(in_ref[slot, :, at])
                turned_ref[slot, at, : 2 * edge] = jnp.concatenate([high, middle], axis=0).T
                turned_ref[slot, at, 2 * edge :] = jnp.concatenate([low, high], axis=0).T

    return kernel_call(
        body, [shaped(slots, pairs, 4 * edge, dtype=jnp.bfloat16)], [blocks], after=after
    )[0]


def dot32(left, right):
    return jnp.dot(left, right, preferred_element_type=jnp.float32)


def gram_parts(rows):
    rank = rows.shape[1]
    high, middle, least = split3(rows)
    both = jnp.concatenate([high, middle], axis=1)
    turned = both.T
    return dot32(turned, both), dot32(turned[:rank], least)


def join_gram(parts):
    square, rest = parts
    rank = rest.shape[0]
    rest = rest + square[:rank, rank:]
    return (square[rank:, rank:] + (rest + rest.T)) + square[:rank, :rank]


def split3(value):
    high = value.astype(jnp.bfloat16)
    rest = value - high.astype(jnp.float32)
    middle = rest.astype(jnp.bfloat16)
    low = (rest - middle.astype(jnp.float32)).astype(jnp.bfloat16)
    return high, middle, low


def second_mode(terms, inverse, spread_blocks, rows, wide_size):
    low = len(terms)
    pairs, edge, rank = rows.shape
    slots = pairs // 2
    slice_rows = edge // wide_size
    chunk = 4

    def tag_of(ref, d, slot, at):
        return ref[d, slots * edge + slot : slots * edge + slot + 1, at : at + 1]

    def body(*refs):
        term_refs = refs[: len(terms)]
        inverse_ref, spread_ref, rows_ref = refs[len(terms) : len(terms) + 3]
        out_refs = refs[len(terms) + 3 : len(terms) + 3 + low]
        held_ref = refs[-1]
        sums = []
        for slot in range(slots):
            total = None
            for m in range(wide_size):
                for other in range(slots):
                    there = tag_of(term_refs[m % low], m // low, other, 0)
                    same = (there == tag_of(term_refs[0], 0, slot, 0)).astype(jnp.float32)
                    here = slice(other * edge, (other + 1) * edge)
                    part = term_refs[m % low][m // low, here, :] * same
                    total = part if total is None else total + part
            sums.append(total)
        aux = product(jnp.concatenate(sums, axis=0), inverse_ref[...])
        for slot in range(slots):
            weight = tag_of(term_refs[0], 0, slot, live_at)
            high, middle, least = split3(aux[slot * edge : (slot + 1) * edge] * weight)
            none = jnp.zeros_like(high)
            stacked = jnp.concatenate(
                [
                    jnp.concatenate([high, high, high, none], axis=0),
                    jnp.concatenate([middle, middle, none, least], axis=0),
                ],
                axis=1,
            )
            rows_i, rows_j = rows_ref[2 * slot], rows_ref[2 * slot + 1]

            def step(index, total_j):
                at = pl.multiple_of(index * (chunk * edge), chunk * edge)
                spread = jnp.dot(
                    spread_ref[slot, pl.ds(at, chunk * edge), :],
                    stacked,
                    preferred_element_type=jnp.float32,
                )
                spread = spread[:, :rank] + spread[:, rank:]
                for inner in range(chunk):
                    part = spread[inner * edge : (inner + 1) * edge]
                    here = index * chunk + inner
                    held_ref[2 * slot, pl.ds(here, 1), :] = jnp.sum(
                        part * rows_j, axis=0, keepdims=True
                    )
                    total_j = total_j + part * rows_ref[2 * slot, pl.ds(here, 1), :]
                return total_j

            held_ref[2 * slot + 1] = lax.fori_loop(
                0, edge // chunk, step, jnp.zeros((edge, rank), jnp.float32), unroll=True
            )
        wide_at = lax.axis_index("wide")
        for place in range(wide_size):
            source = (wide_at ^ place) * slice_rows
            for pair in range(2 * slots):
                out_refs[place % low][place // low, pair] = held_ref[
                    pair, pl.ds(pl.multiple_of(source, slice_rows), slice_rows), :
                ]

    return kernel_call(
        body,
        [shaped(wide_size // low, 2 * slots, slice_rows, rank)] * low,
        list(terms) + [inverse, spread_blocks, rows],
        scratch=[pltpu.VMEM((2 * slots, edge, rank), jnp.float32)],
        about_us=2.5,
    )


def read_coords(terms, slots, edge, axes):
    low = len(terms)
    partners = terms[0].shape[0]

    def body(*refs):
        for j in range(low):
            for d in range(partners):
                tags = refs[j][d, slots * edge : slots * (edge + 1), :axes]
                refs[-1][d * low + j] = tags.astype(jnp.int32)

    return kernel_call(
        body, [shaped(partners * low, slots, axes, dtype=jnp.int32)], list(terms)
    )[0]


def column_gram(coords, terms, inverse, edge, after):
    low = len(terms)
    devices, slots, _ = coords.shape
    rank = inverse.shape[0]
    count = devices * slots

    def body(coord_ref, *refs):
        term_refs = refs[:low]
        inverse_ref, gram_ref, aux_ref = refs[low:]
        wide_at = lax.axis_index("wide")
        aux_ref[...] = jnp.zeros_like(aux_ref)
        blocks_at = [
            coord_ref[wide_at ^ (index // slots), index % slots, 0] for index in range(count)
        ]
        for index in range(count):
            to = jnp.int32(index)
            for earlier in reversed(range(index)):
                to = jnp.where(blocks_at[earlier] == blocks_at[index], earlier, to)
            here = slice(index % slots * edge, (index % slots + 1) * edge)
            place = wide_at ^ (index // slots)
            term = term_refs[0][place // low, here, :]
            for j in range(1, low):
                term = jnp.where(place % low == j, term_refs[j][place // low, here, :], term)
            aux_ref[to] += term
        high, middle, least = split3(inverse_ref[...])
        left_high, left_middle, left_least = split3(aux_ref[...].reshape(count * edge, rank))
        one = jnp.concatenate([high, middle], axis=1)
        aux = dot32(
            jnp.concatenate([left_high, left_middle], axis=1),
            jnp.concatenate([one, one], axis=0),
        )
        aux = (aux[:, :rank] + aux[:, rank:]) + dot32(
            jnp.concatenate([left_least, left_high], axis=1),
            jnp.concatenate([high, least], axis=0),
        )
        aux_ref[...] = aux.reshape(count, edge, rank)
        gram_ref[...] = join_gram(gram_parts(aux))

    return kernel_call(
        body,
        [shaped(rank, rank), shaped(count, edge, rank)],
        [coords] + list(terms) + [inverse],
        scalars=1,
        about_us=0.1,
        after=after,
    )


def own_aux(coords, aux, own_rows, after):
    devices, slots, _ = coords.shape
    count, edge, rank = aux.shape
    grain = min(own_rows, edge)
    per_block = edge // grain
    per_device = own_rows // grain

    def body(coord_ref, aux_ref, out_ref, done_ref):
        done_ref[...] = jnp.zeros_like(done_ref)
        out_ref[...] = jnp.zeros_like(out_ref)
        wide_at = lax.axis_index("wide")
        blocks_at = [
            coord_ref[wide_at ^ (index // slots), index % slots, 0] for index in range(count)
        ]
        for index in range(count):
            first = jnp.bool_(True)
            for earlier in range(index):
                first = first & (blocks_at[earlier] != blocks_at[index])
            for part in range(per_block):
                grain_at = blocks_at[index] * per_block + part

                @pl.when(first & (grain_at // per_device == wide_at))
                def _():
                    out_ref[grain_at % per_device] = aux_ref[
                        index, part * grain : (part + 1) * grain, :
                    ]

    owned, done = kernel_call(
        body,
        [shaped(per_device, grain, rank), shaped(8, rank)],
        [coords, aux],
        scalars=1,
        about_us=0.1,
        after=after,
    )
    return owned.reshape(own_rows, rank), done


def pack_pieces(groups):
    low = len(groups)
    partners = groups[0].shape[0]

    def body(*refs):
        for d in range(partners):
            for j in range(low):
                refs[low + d][j] = refs[j][d]

    return kernel_call(body, [shaped(low, *groups[0].shape[1:])] * partners, list(groups))


def pack_whole(items, after=(), rows=None):
    rows = rows or items[0].shape[0]
    kind = shaped(len(items), rows, *items[0].shape[1:], dtype=items[0].dtype)

    def body(*refs):
        for index, ref in enumerate(refs[:-1]):
            refs[-1][index] = ref[:rows]

    return kernel_call(body, [kind], list(items), after=after)[0]


def with_partners(value, low):
    return [value] + [swap_with(value, "wide", j) for j in range(1, low)]


def add_pieces(coords, pieces, narrow_size, own_blocks, after):
    low, pairs, rows, rank = pieces[0].shape
    part_rows = own_blocks * rows

    def body(coord_ref, *refs):
        narrow_at = lax.axis_index("narrow")
        piece_refs = refs[: len(pieces)]
        out_refs = refs[len(pieces) : len(pieces) + narrow_size]
        held_ref = refs[-1]
        held_ref[...] = jnp.zeros_like(held_ref)
        for d, piece_ref in enumerate(piece_refs):
            for j in range(low):
                for pair in range(pairs):
                    block = coord_ref[d * low + j, pair // 2, 1 + pair % 2]
                    held_ref[block] += piece_ref[j, pair]
        for m, out_ref in enumerate(out_refs):
            owner = narrow_at ^ m
            part = held_ref[pl.ds(owner * own_blocks, own_blocks)]
            out_ref[...] = part.reshape(part_rows, rank)

    return kernel_call(
        body,
        [shaped(part_rows, rank)] * narrow_size,
        [coords] + list(pieces),
        scalars=1,
        after=after,
        scratch=[pltpu.VMEM((narrow_size * own_blocks, rows, rank), jnp.float32)],
    )


def add_parts(parts, after=()):
    def body(*refs):
        total = refs[0][...]
        for ref in refs[1:-1]:
            total = total + ref[...]
        refs[-1][...] = total

    return kernel_call(body, [shaped(*parts[0].shape)], list(parts), after=after)[0]


def solve_rows(parts, inverse, own_blocks):
    low = len(parts)
    partners, part_rows, rank = parts[0].shape
    rows = part_rows // own_blocks

    def body(*refs):
        wide_at = lax.axis_index("wide")
        out_ref = refs[-1]
        for d in range(partners):
            for j in range(low):
                solved = product(refs[j][d], refs[low][...]).reshape(own_blocks, rows, rank)
                place = wide_at ^ (d * low + j)
                for block in range(own_blocks):
                    out_ref[block, place] = solved[block]

    return kernel_call(
        body,
        [shaped(own_blocks, partners * low, rows, rank)],
        list(parts) + [inverse],
        about_us=1.5,
    )[0]


def on_device(blocks, block_coords, block_count, orbital_factor):
    slots, edge = blocks.shape[2:4]
    rank = orbital_factor.shape[1]
    wide_size = lax.axis_size("wide")
    narrow_size = lax.axis_size("narrow")
    low = digits_of(wide_size)[0][1]
    slice_rows = edge // wide_size
    own_blocks = orbital_factor.shape[0] // edge
    own_rows = NP // narrow_size // wide_size

    by_slice = orbital_factor.reshape(own_blocks, wide_size // low, low, slice_rows, rank)
    chip_at = lax.axis_index("wide") // low
    chip_slice = lax.dynamic_index_in_dim(by_slice, chip_at, 1, keepdims=False)
    own_slice = own_part(chip_slice)
    pairs = [send_by_core(chip_slice, [m, m + 1]) for m in range(1, narrow_size - 1, low)]
    single = swap_with(own_slice, "narrow", narrow_size - 1)
    arrived = gather_from(block_coords[0, 0], "wide", skip=1)[1:]
    tags, coords = open_tags(block_coords[0, 0], block_count, [own_slice])
    blocks = stage(blocks[0, 0], [tags])
    coords = pack_whole([coords] + arrived, after=[blocks])
    mine = pack_slices(pairs, single, [coords])
    theirs = swap_with(mine, "wide", 1)
    wanted = pick_pieces(coords, chip_slice, mine, theirs, narrow_size, [])
    pieces = exchange(wanted, "wide", skip=1)

    turned = turn_blocks(blocks, wanted[:1])
    rows, terms = first_mode(tags, pieces, blocks, wide_size, low, [turned])
    inverse_b, gram_b = inverse_of(pieces, None, 1.0, after=[terms])
    terms = pack_whole(gather_from(terms, "wide", skip=1), after=[inverse_b])
    column_terms = with_partners(terms, low)
    all_coords = read_coords(column_terms, slots, edge, block_coords.shape[3])

    groups = second_mode(column_terms, inverse_b, turned, rows, wide_size)
    groups = [groups[0]] + [swap_with(groups[j], "wide", j) for j in range(1, low)]
    packed = pack_pieces(groups)
    pieces = exchange(packed, "wide", skip=1)

    gram, aux = column_gram(all_coords, column_terms, inverse_b, edge, packed[:1])

    sums = add_pieces(all_coords, pieces, narrow_size, own_blocks, [gram])
    parts = exchange(sums, "narrow")
    step = narrow_size // 2
    while step > 1:
        gram = add_parts([gram, swap_with(gram, "narrow", step)], sums[:1])
        step //= 2
    aux_owned, done = own_aux(all_coords, aux, own_rows, sums[:1])
    total = add_parts(parts, [gram, done])
    (inverse_a,) = inverse_of([gram, swap_with(gram, "narrow", step)], gram_b, 2.0, [total])
    totals = pack_whole(gather_from(total, "wide", skip=1), after=[inverse_a])
    orbital_new = solve_rows(with_partners(totals, low), inverse_a, own_blocks)
    return (aux_owned[None], orbital_new.reshape(own_blocks * edge, rank))


def solution(mesh):
    return jax.shard_map(
        on_device,
        mesh=mesh,
        in_specs=(
            P("wide", "narrow", None, None, None),
            P("wide", "narrow", None, None),
            P("wide", "narrow"),
            P("narrow", None),
        ),
        out_specs=(P("narrow", "wide", None), P("narrow", None)),
        check_vma=False,
    )
```

```python
import functools

import jax
import jax.numpy as jnp
from jax import lax
from jax.experimental import pallas as pl
from jax.experimental.pallas import tpu as pltpu
from jax.sharding import PartitionSpec as P

NP = 16384


precise_level = lax.Precision.HIGHEST
in_vmem = pl.BlockSpec(memory_space=pltpu.VMEM)
in_smem = pl.BlockSpec(memory_space=pltpu.SMEM)
live_at = 3
in_hbm = pl.BlockSpec(memory_space=pltpu.HBM)


def product(left, right):
    return jnp.dot(left, right, precision=precise_level, preferred_element_type=jnp.float32)


def kernel_call(body, outputs, operands, scalars=0, scratch=(), about_us=0.3, after=(), far=False):
    after = list(after)

    def whole(*refs):
        body(*refs[: len(operands)], *refs[len(operands) + len(after) :])

    return pl.pallas_call(
        whole,
        out_shape=outputs,
        in_specs=[in_smem] * scalars
        + [in_hbm if far else in_vmem] * (len(operands) - scalars)
        + [pl.BlockSpec(memory_space=pl.ANY)] * len(after),
        out_specs=[in_vmem] * len(outputs),
        scratch_shapes=list(scratch),
        compiler_params=pltpu.CompilerParams(vmem_limit_bytes=24 * 1024 * 1024),
        cost_estimate=pl.CostEstimate(
            flops=int(about_us * 1e6), bytes_accessed=0, transcendentals=0
        ),
    )(*operands, *after)


def shaped(*shape, dtype=jnp.float32):
    return jax.ShapeDtypeStruct(shape, dtype)


def add_tree(items):
    while len(items) > 1:
        items = [items[t] + items[t + 1] for t in range(0, len(items), 2)]
    return items[0]


def digits_of(size):
    digits = []
    stride = 1
    while stride < size:
        left = size // stride
        radix = 2 if left.bit_length() % 2 == 0 else 4
        digits.append((stride, radix))
        stride *= radix
    return digits


def swap_with(value, axis, mask):
    size = lax.axis_size(axis)
    return lax.ppermute(value, axis, [(index, index ^ mask) for index in range(size)])


def send_by_core(value, masks):
    wide_size, narrow_size = lax.axis_size("wide"), lax.axis_size("narrow")
    pairs = [
        (w * narrow_size + n, w * narrow_size + (n ^ masks[w % len(masks)]))
        for w in range(wide_size)
        for n in range(narrow_size)
    ]
    return lax.ppermute(value, ("wide", "narrow"), pairs)


def gather_from(value, axis, skip=0):
    digits = digits_of(lax.axis_size(axis))
    held = {0: value}
    for stride, radix in reversed(digits[skip:]):
        fresh = {}
        for digit in range(1, radix):
            for key, item in held.items():
                fresh[key + digit * stride] = swap_with(item, axis, digit * stride)
        held.update(fresh)
    return [held[key] for key in sorted(held)]


def exchange(items, axis, skip=0):
    digits = digits_of(lax.axis_size(axis))
    unit = digits[skip][0] if skip < len(digits) else 1
    items = list(items)
    for stride, radix in digits[skip:]:
        step = stride // unit
        for digit in range(1, radix):
            at = [key for key in range(len(items)) if key // step % radix == digit]
            if len(at) == 1:
                items[at[0]] = swap_with(items[at[0]], axis, digit * stride)
            else:
                packed = swap_with(jnp.stack([items[key] for key in at]), axis, digit * stride)
                for place, key in enumerate(at):
                    items[key] = packed[place]
    return items


def inverse_of(grams, other, scale, after=()):
    size = grams[0].shape[-1]
    step = 16
    count = size // step
    own = other is None
    operands = list(grams) + ([] if own else [other])
    outputs = [shaped(size, size)] + ([shaped(size, size)] if own else [])

    def body(*refs):
        parts = refs[: len(grams)]
        out_ref = refs[len(operands)]
        left_ref, right_ref = refs[-2:]
        sub = lax.broadcasted_iota(jnp.int32, (step, size), 0)
        lane = lax.broadcasted_iota(jnp.int32, (step, size), 1)
        held = []
        for block in range(count):
            at = slice(step * block, step * block + step)
            total = add_tree([part[pl.ds(part.shape[0] - size + step * block, step), :] for part in parts])
            if own:
                refs[len(operands) + 1][at, :] = total
                held.append(total * total)
            else:
                held.append(scale * total * refs[len(grams)][at, :])

        def splat_lane(value, index):
            return jnp.broadcast_to(value[:, index : index + 1], (step, size))

        def splat_row(value, index):
            return jnp.broadcast_to(value[index : index + 1, :], (step, size))

        for block in range(count):
            at = slice(step * block, step * block + step)
            inside = (lane >= step * block) & (lane < step * block + step)
            upto = lane < step * block + step
            unit = (lane - step * block == sub).astype(jnp.float32)
            pivots = [splat_lane(held[block], step * block + t) for t in range(step)]
            panel = jnp.where(inside, unit, held[block])
            left_ref[at, :] = jnp.where(upto, panel, 0.0)
            for p in range(0, step, 2):
                first, second = sub == p, sub == p + 1
                corner = splat_row(pivots[p], p)
                above, below = splat_row(pivots[p + 1], p), splat_row(pivots[p], p + 1)
                last = splat_row(pivots[p + 1], p + 1)
                scaled = 1.0 / (corner * last - above * below)
                i11, i12, i21, i22 = last * scaled, -above * scaled, -below * scaled, corner * scaled
                one = jnp.where(
                    first, -i11, jnp.where(second, -i21, pivots[p] * i11 + pivots[p + 1] * i21)
                )
                two = jnp.where(
                    first, -i12, jnp.where(second, -i22, pivots[p] * i12 + pivots[p + 1] * i22)
                )

                def clear(value):
                    kept = jnp.where(first | second, 0.0, value)
                    return kept - (one * splat_row(value, p) + two * splat_row(value, p + 1))

                for t in range(p + 2, step):
                    pivots[t] = clear(pivots[t])
                panel = clear(panel)
            right_ref[at, :] = jnp.where(upto, panel, 0.0)
            rows = [splat_row(panel, t) for t in range(step)]
            for index in range(block + 1, count):
                pairs = [splat_lane(held[index], step * block + t) * rows[t] for t in range(step)]
                held[index] = jnp.where(inside, 0.0, held[index]) - add_tree(pairs)
        out_ref[...] = lax.dot_general(
            left_ref[...],
            right_ref[...],
            (((0,), (0,)), ((), ())),
            precision=precise_level,
            preferred_element_type=jnp.float32,
        )

    return kernel_call(
        body,
        outputs,
        operands,
        scratch=[pltpu.VMEM((size, size), jnp.float32)] * 2,
        about_us=3.5,
        after=after,
    )


def own_part(chip_slice):
    own_blocks, low, rows, rank = chip_slice.shape

    def body(in_ref, out_ref):
        core = lax.axis_index("wide") % low
        for block in range(own_blocks):
            out_ref[block] = in_ref[block, core]

    return kernel_call(body, [shaped(own_blocks, rows, rank)], [chip_slice])[0]


def open_tags(coords, count, rank, after):
    slots, axes = coords.shape

    def body(coords_ref, count_ref, tag_ref, out_ref):
        slot_at = lax.broadcasted_iota(jnp.int32, (slots, 1), 0)
        tag_ref[...] = jnp.zeros_like(tag_ref)
        tag_ref[:slots, :axes] = coords_ref[...].astype(jnp.float32)
        tag_ref[:slots, axes : axes + 1] = (slot_at < count_ref[...]).astype(jnp.float32)
        out_ref[...] = coords_ref[...]

    return kernel_call(
        body,
        [shaped(8, rank), shaped(slots, axes, dtype=jnp.int32)],
        [coords, count],
        after=after,
    )


def stage(value, after):
    def body(in_ref, out_ref, sem):
        copy = pltpu.make_async_copy(in_ref, out_ref, sem)
        copy.start()
        copy.wait()

    return kernel_call(
        body,
        [shaped(*value.shape)],
        [value],
        scratch=[pltpu.SemaphoreType.DMA],
        after=after,
        far=True,
    )[0]


def pack_slices(pairs, single, after):
    own_blocks, low, rows, rank = pairs[0].shape if pairs else (single.shape[0], 0, 0, 0)
    _, rows, rank = single.shape
    total = own_blocks * (low * len(pairs) + 1)

    def body(*refs):
        out_ref = refs[-1]
        for index, ref in enumerate(refs[: len(pairs)]):
            at = index * own_blocks * low
            out_ref[at : at + own_blocks * low] = ref[...].reshape(own_blocks * low, rows, rank)
        out_ref[total - own_blocks :] = refs[len(pairs)][...]

    return kernel_call(
        body, [shaped(total, rows, rank)], list(pairs) + [single], after=after
    )[0]


def pick_pieces(coords, own, mine, theirs, narrow_size, after):
    own_blocks, low, rows, rank = own.shape
    partners, slots, _ = coords.shape
    piece_rows = slots * 2 * low * rows

    def body(there_ref, own_ref, mine_ref, theirs_ref, *refs):
        out_refs, coord_ref, sem = refs[:partners], refs[partners], refs[partners + 1]
        narrow_at = lax.axis_index("narrow")
        core = lax.axis_index("wide") % low
        copy = pltpu.make_async_copy(there_ref, coord_ref, sem)
        copy.start()
        here, there = mine_ref[...].reshape(-1, rank), theirs_ref[...].reshape(-1, rank)
        rows_of = [jnp.where(core == j, here, there) for j in range(low)]
        gram = join_gram(
            gram_parts(jnp.concatenate([own_ref[...].reshape(-1, rank)] + rows_of, axis=0))
        )
        for out_ref in out_refs:
            out_ref[piece_rows:, :] = gram
        copy.wait()
        for d, out_ref in enumerate(out_refs):
            for pair in range(slots * 2):
                block = coord_ref[d, pair // 2, 1 + pair % 2]
                owner = (block // own_blocks) ^ narrow_at
                local = block % own_blocks
                before = jnp.maximum(owner, 1) - 1
                last = before == narrow_size - 2
                for j in range(low):
                    slice_at = core ^ j
                    holder = jnp.where(last, slice_at, before % low)
                    at = jnp.where(
                        last,
                        (narrow_size - 2) * own_blocks + local,
                        (before // low * own_blocks + local) * low + slice_at,
                    )
                    away = jnp.where(holder == core, mine_ref[at], theirs_ref[at])
                    to = (pair * low + j) * rows
                    out_ref[to : to + rows, :] = jnp.where(
                        owner == 0, own_ref[local, slice_at], away
                    )

    return kernel_call(
        body,
        [shaped(piece_rows + rank, rank)] * partners,
        [coords, own, mine, theirs],
        scratch=[pltpu.SMEM(coords.shape, jnp.int32), pltpu.SemaphoreType.DMA],
        after=after,
    )


def first_mode(tags, pieces, spread, wide_size, low):
    rank = pieces[0].shape[1]
    slots, _, width = spread.shape
    edge = width // 4
    pairs = 2 * slots
    slice_rows = edge // wide_size
    chunk = 4

    def body(tag_ref, *refs):
        piece_refs = refs[: len(pieces)]
        spread_ref, rows_ref, term_ref, held_ref = refs[len(pieces) :]
        term_ref[slots * edge :, :] = tag_ref[...]
        wide_at = lax.axis_index("wide")
        for d, piece_ref in enumerate(piece_refs):
            for j in range(low):
                place = wide_at ^ (d * low + j)
                for pair in range(pairs):
                    at = (pair * low + j) * slice_rows
                    held_ref[pair, place] = piece_ref[at : at + slice_rows, :]
        rows_ref[...] = held_ref[...].reshape(pairs, edge, rank)
        for slot in range(slots):
            stacked = stack_parts(rows_ref[2 * slot + 1])

            def step(index, total):
                at = pl.multiple_of(index * (chunk * edge), chunk * edge)
                product = dot32(spread_ref[slot, pl.ds(at, chunk * edge), :], stacked)
                product = product[:, :rank] + product[:, rank:]
                for inner in range(chunk):
                    row = rows_ref[2 * slot, pl.ds(index * chunk + inner, 1), :]
                    total = total + product[inner * edge : (inner + 1) * edge] * row
                return total

            total = lax.fori_loop(
                0, edge // chunk, step, jnp.zeros((edge, rank), jnp.float32), unroll=True
            )
            live = tag_ref[slot : slot + 1, live_at : live_at + 1]
            term_ref[slot * edge : (slot + 1) * edge, :] = total * live

    return kernel_call(
        body,
        [shaped(pairs, edge, rank), shaped(slots * edge + tags.shape[0], rank)],
        [tags] + list(pieces) + [spread],
        scratch=[pltpu.VMEM((pairs, wide_size, slice_rows, rank), jnp.float32)],
        about_us=3.0,
    )


def split_blocks(blocks, after):
    slots, edge, pairs = blocks.shape
    turn = 512
    lanes = 2 * edge

    def body(in_ref, spread_ref, turned_ref):
        left = lax.broadcasted_iota(jnp.int32, (edge, lanes), 1) < edge

        def roll(value):
            return pltpu.roll(value, edge, 1)

        for slot in range(slots):

            @pl.loop(0, pairs // turn)
            def _(index):
                at = pl.multiple_of(index * turn, turn)
                parts = []
                for inner in range(turn // lanes):
                    value = in_ref[slot, :, pl.ds(at + inner * lanes, lanes)]
                    high = value.astype(jnp.bfloat16).astype(jnp.float32)
                    rest = value - high
                    middle = rest.astype(jnp.bfloat16).astype(jnp.float32)
                    low = rest - middle
                    other_high, other_middle, other_low = roll(high), roll(middle), roll(low)
                    rows = [
                        [jnp.where(left, high, other_middle), jnp.where(left, low, other_high)],
                        [jnp.where(left, other_high, middle), jnp.where(left, other_low, high)],
                    ]
                    row_at = pl.multiple_of((at // lanes + inner) * lanes, lanes)
                    for half in range(2):
                        spread_ref[slot, pl.ds(row_at + half * edge, edge), :] = jnp.concatenate(
                            rows[half], axis=1
                        ).astype(jnp.bfloat16)
                    parts.append([item.astype(jnp.bfloat16) for item in (high, middle, low)])
                high, middle, low = [jnp.concatenate(item, axis=1) for item in zip(*parts)]
                here = pl.ds(at, turn)
                turned_ref[slot, here, : 2 * edge] = jnp.concatenate([high, middle], axis=0).T
                turned_ref[slot, here, 2 * edge :] = jnp.concatenate([low, high], axis=0).T

    kind = shaped(slots, pairs, 4 * edge, dtype=jnp.bfloat16)
    return kernel_call(body, [kind, kind], [blocks], after=after)


def dot32(left, right):
    return jnp.dot(left, right, preferred_element_type=jnp.float32)


def times(rows, matrix):
    rank = matrix.shape[1]
    high, middle, least = split3(matrix)
    left_high, left_middle, left_least = split3(rows)
    one = jnp.concatenate([high, middle], axis=1)
    wide = dot32(
        jnp.concatenate([left_high, left_middle], axis=1), jnp.concatenate([one, one], axis=0)
    )
    thin = dot32(
        jnp.concatenate([left_least, left_high], axis=1), jnp.concatenate([high, least], axis=0)
    )
    return (thin + wide[:, rank:]) + wide[:, :rank]


def stack_parts(matrix):
    high, middle, least = split3(matrix)
    none = jnp.zeros_like(high)
    return jnp.concatenate(
        [
            jnp.concatenate([high, high, high, none], axis=0),
            jnp.concatenate([middle, middle, none, least], axis=0),
        ],
        axis=1,
    )


def gram_parts(rows):
    rank = rows.shape[1]
    high, middle, least = split3(rows)
    both = jnp.concatenate([high, middle], axis=1)
    turned = both.T
    return dot32(turned, both), dot32(turned[:rank], least)


def join_gram(parts):
    square, rest = parts
    rank = rest.shape[0]
    rest = rest + square[:rank, rank:]
    return (square[rank:, rank:] + (rest + rest.T)) + square[:rank, :rank]


def split3(value):
    high = value.astype(jnp.bfloat16)
    rest = value - high.astype(jnp.float32)
    middle = rest.astype(jnp.bfloat16)
    low = (rest - middle.astype(jnp.float32)).astype(jnp.bfloat16)
    return high, middle, low


def second_mode(terms, inverse, spread_blocks, rows, wide_size):
    low = len(terms)
    pairs, edge, rank = rows.shape
    slots = pairs // 2
    slice_rows = edge // wide_size
    chunk = 4

    def tag_of(ref, d, slot, at):
        return ref[d, slots * edge + slot : slots * edge + slot + 1, at : at + 1]

    def body(*refs):
        term_refs = refs[: len(terms)]
        inverse_ref, spread_ref, rows_ref = refs[len(terms) : len(terms) + 3]
        out_refs = refs[len(terms) + 3 : len(terms) + 3 + low]
        held_ref = refs[-1]
        sums = []
        for slot in range(slots):
            total = None
            for m in range(wide_size):
                for other in range(slots):
                    there = tag_of(term_refs[m % low], m // low, other, 0)
                    same = (there == tag_of(term_refs[0], 0, slot, 0)).astype(jnp.float32)
                    here = slice(other * edge, (other + 1) * edge)
                    part = term_refs[m % low][m // low, here, :] * same
                    total = part if total is None else total + part
            sums.append(total)
        aux = times(jnp.concatenate(sums, axis=0), inverse_ref[...])
        for slot in range(slots):
            weight = tag_of(term_refs[0], 0, slot, live_at)
            stacked = stack_parts(aux[slot * edge : (slot + 1) * edge] * weight)
            rows_i, rows_j = rows_ref[2 * slot], rows_ref[2 * slot + 1]

            def step(index, total_j):
                at = pl.multiple_of(index * (chunk * edge), chunk * edge)
                spread = jnp.dot(
                    spread_ref[slot, pl.ds(at, chunk * edge), :],
                    stacked,
                    preferred_element_type=jnp.float32,
                )
                spread = spread[:, :rank] + spread[:, rank:]
                for inner in range(chunk):
                    part = spread[inner * edge : (inner + 1) * edge]
                    here = index * chunk + inner
                    held_ref[2 * slot, pl.ds(here, 1), :] = jnp.sum(
                        part * rows_j, axis=0, keepdims=True
                    )
                    total_j = total_j + part * rows_ref[2 * slot, pl.ds(here, 1), :]
                return total_j

            held_ref[2 * slot + 1] = lax.fori_loop(
                0, edge // chunk, step, jnp.zeros((edge, rank), jnp.float32), unroll=True
            )
        wide_at = lax.axis_index("wide")
        for place in range(wide_size):
            source = (wide_at ^ place) * slice_rows
            for pair in range(2 * slots):
                out_refs[place % low][place // low, pair] = held_ref[
                    pair, pl.ds(pl.multiple_of(source, slice_rows), slice_rows), :
                ]

    return kernel_call(
        body,
        [shaped(wide_size // low, 2 * slots, slice_rows, rank)] * low,
        list(terms) + [inverse, spread_blocks, rows],
        scratch=[pltpu.VMEM((2 * slots, edge, rank), jnp.float32)],
        about_us=2.5,
    )


def read_coords(terms, slots, edge, axes):
    low = len(terms)
    partners = terms[0].shape[0]

    def body(*refs):
        for j in range(low):
            for d in range(partners):
                tags = refs[j][d, slots * edge : slots * (edge + 1), :axes]
                refs[-1][d * low + j] = tags.astype(jnp.int32)

    return kernel_call(
        body, [shaped(partners * low, slots, axes, dtype=jnp.int32)], list(terms)
    )[0]


def column_gram(coords, terms, inverse, edge, after):
    low = len(terms)
    devices, slots, _ = coords.shape
    rank = inverse.shape[0]
    count = devices * slots

    def body(coord_ref, *refs):
        term_refs = refs[:low]
        inverse_ref, gram_ref, aux_ref = refs[low:]
        wide_at = lax.axis_index("wide")
        aux_ref[...] = jnp.zeros_like(aux_ref)
        blocks_at = [
            coord_ref[wide_at ^ (index // slots), index % slots, 0] for index in range(count)
        ]
        for index in range(count):
            to = jnp.int32(index)
            for earlier in reversed(range(index)):
                to = jnp.where(blocks_at[earlier] == blocks_at[index], earlier, to)
            here = slice(index % slots * edge, (index % slots + 1) * edge)
            place = wide_at ^ (index // slots)
            term = term_refs[0][place // low, here, :]
            for j in range(1, low):
                term = jnp.where(place % low == j, term_refs[j][place // low, here, :], term)
            aux_ref[to] += term
        aux = times(aux_ref[...].reshape(count * edge, rank), inverse_ref[...])
        aux_ref[...] = aux.reshape(count, edge, rank)
        gram_ref[...] = join_gram(gram_parts(aux))

    return kernel_call(
        body,
        [shaped(rank, rank), shaped(count, edge, rank)],
        [coords] + list(terms) + [inverse],
        scalars=1,
        about_us=0.1,
        after=after,
    )


def own_aux(coords, aux, own_rows, after):
    devices, slots, _ = coords.shape
    count, edge, rank = aux.shape
    grain = min(own_rows, edge)
    per_block = edge // grain
    per_device = own_rows // grain

    def body(coord_ref, aux_ref, out_ref, done_ref):
        done_ref[...] = jnp.zeros_like(done_ref)
        out_ref[...] = jnp.zeros_like(out_ref)
        wide_at = lax.axis_index("wide")
        blocks_at = [
            coord_ref[wide_at ^ (index // slots), index % slots, 0] for index in range(count)
        ]
        for index in range(count):
            first = jnp.bool_(True)
            for earlier in range(index):
                first = first & (blocks_at[earlier] != blocks_at[index])
            for part in range(per_block):
                grain_at = blocks_at[index] * per_block + part

                @pl.when(first & (grain_at // per_device == wide_at))
                def _():
                    out_ref[grain_at % per_device] = aux_ref[
                        index, part * grain : (part + 1) * grain, :
                    ]

    owned, done = kernel_call(
        body,
        [shaped(per_device, grain, rank), shaped(8, rank)],
        [coords, aux],
        scalars=1,
        about_us=0.1,
        after=after,
    )
    return owned.reshape(own_rows, rank), done


def pack_pieces(groups):
    low = len(groups)
    partners = groups[0].shape[0]

    def body(*refs):
        for d in range(partners):
            for j in range(low):
                refs[low + d][j] = refs[j][d]

    return kernel_call(body, [shaped(low, *groups[0].shape[1:])] * partners, list(groups))


def pack_whole(items, after=(), rows=None):
    rows = rows or items[0].shape[0]
    kind = shaped(len(items), rows, *items[0].shape[1:], dtype=items[0].dtype)

    def body(*refs):
        for index, ref in enumerate(refs[:-1]):
            refs[-1][index] = ref[:rows]

    return kernel_call(body, [kind], list(items), after=after)[0]


def with_partners(value, low):
    return [value] + [swap_with(value, "wide", j) for j in range(1, low)]


def plan_sums(coords, rows, narrow_size, own_blocks, after):
    devices, slots, _ = coords.shape
    count = devices * slots * 2
    lanes = min(count * rows, 128)

    def body(coord_ref, out_ref, held_ref):
        narrow_at = lax.axis_index("narrow")
        held_ref[...] = jnp.zeros_like(held_ref)
        ahead = lax.broadcasted_iota(jnp.int32, (rows, lanes), 1) - lax.broadcasted_iota(
            jnp.int32, (rows, lanes), 0
        )
        for index in range(count):
            pair = index % (2 * slots)
            block = coord_ref[index // (2 * slots), pair // 2, 1 + pair % 2]
            to = ((block // own_blocks) ^ narrow_at) * own_blocks + block % own_blocks
            at = index * rows // lanes * lanes
            held_ref[to, :, at : at + lanes] += (ahead == index * rows - at).astype(jnp.float32)
        out_ref[...] = held_ref[...].reshape(out_ref.shape).astype(jnp.bfloat16)

    total = narrow_size * own_blocks
    return kernel_call(
        body,
        [shaped(total * rows, count * rows, dtype=jnp.bfloat16)],
        [coords],
        scalars=1,
        scratch=[pltpu.VMEM((total, rows, count * rows), jnp.float32)],
        after=after,
    )[0]


def add_pieces(plan, pieces, narrow_size, after):
    low, pairs, rows, rank = pieces[0].shape
    part_rows = plan.shape[0] // narrow_size

    def body(plan_ref, *refs):
        terms = jnp.concatenate(
            [ref[...].reshape(low * pairs * rows, rank) for ref in refs[: len(pieces)]], axis=0
        )
        high, middle, least = split3(terms)
        wide = dot32(plan_ref[...], jnp.concatenate([high, middle], axis=1))
        sums = (dot32(plan_ref[...], least) + wide[:, rank:]) + wide[:, :rank]
        for m, out_ref in enumerate(refs[len(pieces) :]):
            out_ref[...] = sums[m * part_rows : (m + 1) * part_rows]

    return kernel_call(
        body, [shaped(part_rows, rank)] * narrow_size, [plan] + list(pieces), after=after
    )


def add_parts(parts, after=()):
    def body(*refs):
        total = refs[0][...]
        for ref in refs[1:-1]:
            total = total + ref[...]
        refs[-1][...] = total

    return kernel_call(body, [shaped(*parts[0].shape)], list(parts), after=after)[0]


def solve_rows(parts, inverse):
    rows, rank = parts[0].shape
    count = len(parts)

    def body(*refs):
        solved = times(
            jnp.concatenate([ref[...] for ref in refs[:count]], axis=0), refs[count][...]
        )
        refs[-1][...] = solved.reshape(count, rows, rank)

    return kernel_call(body, [shaped(count, rows, rank)], list(parts) + [inverse])[0]


def lay_rows(parts, own_blocks):
    low = len(parts)
    partners, part_rows, rank = parts[0].shape
    rows = part_rows // own_blocks

    def body(*refs):
        wide_at = lax.axis_index("wide")
        for d in range(partners):
            for j in range(low):
                place = wide_at ^ (d * low + j)
                for block in range(own_blocks):
                    refs[-1][block, place] = refs[j][d, block * rows : (block + 1) * rows, :]

    return kernel_call(body, [shaped(own_blocks, partners * low, rows, rank)], list(parts))[0]


def on_device(blocks, block_coords, block_count, orbital_factor):
    slots, edge = blocks.shape[2:4]
    rank = orbital_factor.shape[1]
    wide_size = lax.axis_size("wide")
    narrow_size = lax.axis_size("narrow")
    low = digits_of(wide_size)[0][1]
    slice_rows = edge // wide_size
    own_blocks = orbital_factor.shape[0] // edge
    own_rows = NP // narrow_size // wide_size

    by_slice = orbital_factor.reshape(own_blocks, wide_size // low, low, slice_rows, rank)
    chip_at = lax.axis_index("wide") // low
    chip_slice = lax.dynamic_index_in_dim(by_slice, chip_at, 1, keepdims=False)
    own_slice = own_part(chip_slice)
    pairs = [send_by_core(chip_slice, [m, m + 1]) for m in range(1, narrow_size - 1, low)]
    single = swap_with(own_slice, "narrow", narrow_size - 1)
    arrived = gather_from(block_coords[0, 0], "wide", skip=1)[1:]
    blocks = stage(blocks[0, 0], [own_slice])
    mine = pack_slices(pairs, single, arrived + [blocks])
    theirs = swap_with(mine, "wide", 1)
    tags, coords = open_tags(block_coords[0, 0], block_count, rank, [mine])
    coords = pack_whole([coords] + arrived)
    wanted = pick_pieces(coords, chip_slice, mine, theirs, narrow_size, [])
    pieces = exchange(wanted, "wide", skip=1)

    spread, turned = split_blocks(blocks, wanted[:1])
    rows, terms = first_mode(tags, pieces, spread, wide_size, low)
    inverse_b, gram_b = inverse_of(pieces, None, 1.0, after=[terms])
    terms = pack_whole(gather_from(terms, "wide", skip=1), after=[inverse_b])
    column_terms = with_partners(terms, low)
    all_coords = read_coords(column_terms, slots, edge, block_coords.shape[3])

    groups = second_mode(column_terms, inverse_b, turned, rows, wide_size)
    groups = [groups[0]] + [swap_with(groups[j], "wide", j) for j in range(1, low)]
    packed = pack_pieces(groups)
    pieces = exchange(packed, "wide", skip=1)

    gram, aux = column_gram(all_coords, column_terms, inverse_b, edge, packed[:1])

    plan = plan_sums(all_coords, slice_rows, narrow_size, own_blocks, [gram])
    sums = add_pieces(plan, pieces, narrow_size, [])
    parts = exchange(sums, "narrow")
    step = narrow_size // 2
    while step > 1:
        gram = add_parts([gram, swap_with(gram, "narrow", step)], sums[:1])
        step //= 2
    aux_owned, done = own_aux(all_coords, aux, own_rows, sums[:1])
    total = add_parts(parts, [gram, done])
    (inverse_a,) = inverse_of([gram, swap_with(gram, "narrow", step)], gram_b, 2.0, [total])
    solved = solve_rows(gather_from(total, "wide", skip=1), inverse_a)
    orbital_new = lay_rows(with_partners(solved, low), own_blocks)
    return (aux_owned[None], orbital_new.reshape(own_blocks * edge, rank))


def solution(mesh):
    return jax.shard_map(
        on_device,
        mesh=mesh,
        in_specs=(
            P("wide", "narrow", None, None, None),
            P("wide", "narrow", None, None),
            P("wide", "narrow"),
            P("narrow", None),
        ),
        out_specs=(P("narrow", "wide", None), P("narrow", None)),
        check_vma=False,
    )
```

```python
import functools

import jax
import jax.numpy as jnp
from jax import lax
from jax.experimental import pallas as pl
from jax.experimental.pallas import tpu as pltpu
from jax.sharding import PartitionSpec as P

NP = 16384


precise_level = lax.Precision.HIGHEST
in_vmem = pl.BlockSpec(memory_space=pltpu.VMEM)
in_smem = pl.BlockSpec(memory_space=pltpu.SMEM)
live_at = 3
in_hbm = pl.BlockSpec(memory_space=pltpu.HBM)


def product(left, right):
    return jnp.dot(left, right, precision=precise_level, preferred_element_type=jnp.float32)


def kernel_call(body, outputs, operands, scalars=0, scratch=(), about_us=0.3, after=(), far=False):
    after = list(after)

    def whole(*refs):
        body(*refs[: len(operands)], *refs[len(operands) + len(after) :])

    return pl.pallas_call(
        whole,
        out_shape=outputs,
        in_specs=[in_smem] * scalars
        + [in_hbm if far else in_vmem] * (len(operands) - scalars)
        + [pl.BlockSpec(memory_space=pl.ANY)] * len(after),
        out_specs=[in_vmem] * len(outputs),
        scratch_shapes=list(scratch),
        compiler_params=pltpu.CompilerParams(vmem_limit_bytes=24 * 1024 * 1024),
        cost_estimate=pl.CostEstimate(
            flops=int(about_us * 1e6), bytes_accessed=0, transcendentals=0
        ),
    )(*operands, *after)


def shaped(*shape, dtype=jnp.float32):
    return jax.ShapeDtypeStruct(shape, dtype)


def add_tree(items):
    while len(items) > 1:
        items = [items[t] + items[t + 1] for t in range(0, len(items), 2)]
    return items[0]


def digits_of(size):
    digits = []
    stride = 1
    while stride < size:
        left = size // stride
        radix = 2 if left.bit_length() % 2 == 0 else 4
        digits.append((stride, radix))
        stride *= radix
    return digits


def swap_with(value, axis, mask):
    size = lax.axis_size(axis)
    return lax.ppermute(value, axis, [(index, index ^ mask) for index in range(size)])


def send_by_core(value, masks):
    wide_size, narrow_size = lax.axis_size("wide"), lax.axis_size("narrow")
    pairs = [
        (w * narrow_size + n, w * narrow_size + (n ^ masks[w % len(masks)]))
        for w in range(wide_size)
        for n in range(narrow_size)
    ]
    return lax.ppermute(value, ("wide", "narrow"), pairs)


def gather_from(value, axis, skip=0):
    digits = digits_of(lax.axis_size(axis))
    held = {0: value}
    for stride, radix in reversed(digits[skip:]):
        fresh = {}
        for digit in reversed(range(1, radix)):
            for key, item in held.items():
                fresh[key + digit * stride] = swap_with(item, axis, digit * stride)
        held.update(fresh)
    return [held[key] for key in sorted(held)]


def exchange(items, axis, skip=0):
    digits = digits_of(lax.axis_size(axis))
    unit = digits[skip][0] if skip < len(digits) else 1
    items = list(items)
    for stride, radix in digits[skip:]:
        step = stride // unit
        for digit in reversed(range(1, radix)):
            at = [key for key in range(len(items)) if key // step % radix == digit]
            if len(at) == 1:
                items[at[0]] = swap_with(items[at[0]], axis, digit * stride)
            else:
                packed = swap_with(jnp.stack([items[key] for key in at]), axis, digit * stride)
                for place, key in enumerate(at):
                    items[key] = packed[place]
    return items


def eliminate(held, left_ref, right_ref, blocks):
    step, size = held[0].shape
    sub = lax.broadcasted_iota(jnp.int32, (step, size), 0)
    lane = lax.broadcasted_iota(jnp.int32, (step, size), 1)

    def splat_lane(value, index):
        return jnp.broadcast_to(value[:, index : index + 1], (step, size))

    def splat_row(value, index):
        return jnp.broadcast_to(value[index : index + 1, :], (step, size))

    for block in blocks:
        at = slice(step * block, step * block + step)
        inside = (lane >= step * block) & (lane < step * block + step)
        upto = lane < step * block + step
        unit = (lane - step * block == sub).astype(jnp.float32)
        pivots = [splat_lane(held[block], step * block + t) for t in range(step)]
        panel = jnp.where(inside, unit, held[block])
        left_ref[at, :] = jnp.where(upto, panel, 0.0)
        for p in range(0, step, 2):
            first, second = sub == p, sub == p + 1
            corner = splat_row(pivots[p], p)
            above, below = splat_row(pivots[p + 1], p), splat_row(pivots[p], p + 1)
            last = splat_row(pivots[p + 1], p + 1)
            scaled = 1.0 / (corner * last - above * below)
            i11, i12, i21, i22 = last * scaled, -above * scaled, -below * scaled, corner * scaled
            one = jnp.where(
                first, -i11, jnp.where(second, -i21, pivots[p] * i11 + pivots[p + 1] * i21)
            )
            two = jnp.where(
                first, -i12, jnp.where(second, -i22, pivots[p] * i12 + pivots[p + 1] * i22)
            )

            def clear(value):
                kept = jnp.where(first | second, 0.0, value)
                return kept - (one * splat_row(value, p) + two * splat_row(value, p + 1))

            for t in range(p + 2, step):
                pivots[t] = clear(pivots[t])
            panel = clear(panel)
        right_ref[at, :] = jnp.where(upto, panel, 0.0)
        rows = [splat_row(panel, t) for t in range(step)]
        for index in range(block + 1, len(held)):
            pairs = [splat_lane(held[index], step * block + t) * rows[t] for t in range(step)]
            held[index] = jnp.where(inside, 0.0, held[index]) - add_tree(pairs)
    return held


pivot_rows = 16


def start_inverse(grams, other, scale, after):
    size = grams[0].shape[-1]
    step = pivot_rows
    count = size // step
    own = other is None
    operands = list(grams) + ([] if own else [other])

    def body(*refs):
        parts, refs = refs[: len(grams)], refs[len(grams) :]
        held = []
        for block in range(count):
            at = slice(step * block, step * block + step)
            if own:
                half = size // 2
                here = slice(step * block % half, step * block % half + step)
                core = lax.axis_index("wide") % 2
                total = jnp.where(
                    core == step * block // half, parts[0][here, :], parts[1][here, :]
                )
                refs[3][at, :] = total
                held.append(total * total)
            else:
                total = add_tree([part[at, :] for part in parts])
                held.append(scale * total * refs[0][at, :])
        held_ref, left_ref, right_ref = refs[:3] if own else refs[1:]
        held = eliminate(held, left_ref, right_ref, range(count // 2))
        for block in range(count):
            at = slice(step * block, step * block + step)
            held_ref[at, :] = held[block]
            if block >= count // 2:
                left_ref[at, :] = jnp.zeros_like(held[block])
                right_ref[at, :] = jnp.zeros_like(held[block])

    outputs = [shaped(size, size)] * (4 if own else 3)
    return kernel_call(body, outputs, operands, about_us=1.8, after=after)


def end_inverse(held, left, right, after):
    size = held.shape[0]
    step = pivot_rows
    count = size // step

    def body(held_ref, left_in, right_in, out_ref, left_ref, right_ref):
        half = size // 2
        left_ref[:half, :] = left_in[:half, :]
        right_ref[:half, :] = right_in[:half, :]
        rows = [held_ref[step * block : step * block + step, :] for block in range(count)]
        eliminate(rows, left_ref, right_ref, range(count // 2, count))
        out_ref[...] = lax.dot_general(
            left_ref[...],
            right_ref[...],
            (((0,), (0,)), ((), ())),
            precision=precise_level,
            preferred_element_type=jnp.float32,
        )

    return kernel_call(
        body,
        [shaped(size, size)],
        [held, left, right],
        scratch=[pltpu.VMEM((size, size), jnp.float32)] * 2,
        about_us=1.6,
        after=after,
    )[0]


def own_part(chip_slice):
    own_blocks, low, rows, rank = chip_slice.shape

    def body(in_ref, out_ref):
        core = lax.axis_index("wide") % low
        for block in range(own_blocks):
            out_ref[block] = in_ref[block, core]

    return kernel_call(body, [shaped(own_blocks, rows, rank)], [chip_slice])[0]


def open_tags(coords, count, rank, after):
    slots, axes = coords.shape

    def body(coords_ref, count_ref, tag_ref, out_ref):
        slot_at = lax.broadcasted_iota(jnp.int32, (slots, 1), 0)
        tag_ref[...] = jnp.zeros_like(tag_ref)
        tag_ref[:slots, :axes] = coords_ref[...].astype(jnp.float32)
        tag_ref[:slots, axes : axes + 1] = (slot_at < count_ref[...]).astype(jnp.float32)
        out_ref[...] = coords_ref[...]

    return kernel_call(
        body,
        [shaped(8, rank), shaped(slots, axes, dtype=jnp.int32)],
        [coords, count],
        after=after,
    )


def stage(value, after):
    def body(in_ref, out_ref, sem):
        copy = pltpu.make_async_copy(in_ref, out_ref, sem)
        copy.start()
        copy.wait()

    return kernel_call(
        body,
        [shaped(*value.shape)],
        [value],
        scratch=[pltpu.SemaphoreType.DMA],
        after=after,
        far=True,
    )[0]


def pack_slices(pairs, single, after):
    own_blocks, low, rows, rank = pairs[0].shape if pairs else (single.shape[0], 0, 0, 0)
    _, rows, rank = single.shape
    total = own_blocks * (low * len(pairs) + 1)

    def body(*refs):
        out_ref = refs[-1]
        for index, ref in enumerate(refs[: len(pairs)]):
            at = index * own_blocks * low
            out_ref[at : at + own_blocks * low] = ref[...].reshape(own_blocks * low, rows, rank)
        out_ref[total - own_blocks :] = refs[len(pairs)][...]

    return kernel_call(
        body, [shaped(total, rows, rank)], list(pairs) + [single], after=after
    )[0]


def pick_pieces(coords, own, mine, theirs, narrow_size, after):
    own_blocks, low, rows, rank = own.shape
    partners, slots, _ = coords.shape
    piece_rows = slots * 2 * low * rows
    share = rank // low

    def body(there_ref, own_ref, mine_ref, theirs_ref, *refs):
        out_refs, (coord_ref, gram_ref, sem) = refs[:partners], refs[partners:]
        narrow_at = lax.axis_index("narrow")
        core = lax.axis_index("wide") % low
        copy = pltpu.make_async_copy(there_ref, coord_ref, sem)
        copy.start()
        here, there = mine_ref[...].reshape(-1, rank), theirs_ref[...].reshape(-1, rank)
        rows_of = [jnp.where(core == j, here, there) for j in range(low)]
        gram_ref[...] = join_gram(
            gram_parts(jnp.concatenate([own_ref[...].reshape(-1, rank)] + rows_of, axis=0))
        )
        for out_ref in out_refs:
            out_ref[piece_rows:, :] = gram_ref[pl.ds(pl.multiple_of(core * share, share), share), :]
        copy.wait()
        for d, out_ref in enumerate(out_refs):
            for pair in range(slots * 2):
                block = coord_ref[d, pair // 2, 1 + pair % 2]
                owner = (block // own_blocks) ^ narrow_at
                local = block % own_blocks
                before = jnp.maximum(owner, 1) - 1
                last = before == narrow_size - 2
                for j in range(low):
                    slice_at = core ^ j
                    holder = jnp.where(last, slice_at, before % low)
                    at = jnp.where(
                        last,
                        (narrow_size - 2) * own_blocks + local,
                        (before // low * own_blocks + local) * low + slice_at,
                    )
                    away = jnp.where(holder == core, mine_ref[at], theirs_ref[at])
                    to = (pair * low + j) * rows
                    out_ref[to : to + rows, :] = jnp.where(
                        owner == 0, own_ref[local, slice_at], away
                    )

    return kernel_call(
        body,
        [shaped(piece_rows + share, rank)] * partners,
        [coords, own, mine, theirs],
        scratch=[
            pltpu.SMEM(coords.shape, jnp.int32),
            pltpu.VMEM((rank, rank), jnp.float32),
            pltpu.SemaphoreType.DMA,
        ],
        after=after,
    )


def first_mode(tags, pieces, spread, wide_size, low, after):
    rank = pieces[0].shape[1]
    slots, _, width = spread.shape
    edge = width // 4
    pairs = 2 * slots
    slice_rows = edge // wide_size
    chunk = 4

    def body(tag_ref, *refs):
        piece_refs = refs[: len(pieces)]
        spread_ref, rows_ref, term_ref, held_ref = refs[len(pieces) :]
        term_ref[slots * edge :, :] = tag_ref[...]
        wide_at = lax.axis_index("wide")
        for d, piece_ref in enumerate(piece_refs):
            for j in range(low):
                place = wide_at ^ (d * low + j)
                for pair in range(pairs):
                    at = (pair * low + j) * slice_rows
                    held_ref[pair, place] = piece_ref[at : at + slice_rows, :]
        rows_ref[...] = held_ref[...].reshape(pairs, edge, rank)
        for slot in range(slots):
            stacked = stack_parts(rows_ref[2 * slot + 1])

            def step(index, total):
                at = pl.multiple_of(index * (chunk * edge), chunk * edge)
                product = dot32(spread_ref[slot, pl.ds(at, chunk * edge), :], stacked)
                product = product[:, :rank] + product[:, rank:]
                for inner in range(chunk):
                    row = rows_ref[2 * slot, pl.ds(index * chunk + inner, 1), :]
                    total = total + product[inner * edge : (inner + 1) * edge] * row
                return total

            total = lax.fori_loop(
                0, edge // chunk, step, jnp.zeros((edge, rank), jnp.float32), unroll=True
            )
            live = tag_ref[slot : slot + 1, live_at : live_at + 1]
            term_ref[slot * edge : (slot + 1) * edge, :] = total * live

    return kernel_call(
        body,
        [shaped(pairs, edge, rank), shaped(slots * edge + tags.shape[0], rank)],
        [tags] + list(pieces) + [spread],
        scratch=[pltpu.VMEM((pairs, wide_size, slice_rows, rank), jnp.float32)],
        about_us=3.0,
        after=after,
    )


def split_blocks(blocks, after):
    slots, edge, pairs = blocks.shape
    turn = 512
    lanes = 2 * edge

    def body(in_ref, spread_ref, turned_ref):
        left = lax.broadcasted_iota(jnp.int32, (edge, lanes), 1) < edge

        def roll(value):
            return pltpu.roll(value, edge, 1)

        for slot in range(slots):

            @pl.loop(0, pairs // turn)
            def _(index):
                at = pl.multiple_of(index * turn, turn)
                parts = []
                for inner in range(turn // lanes):
                    value = in_ref[slot, :, pl.ds(at + inner * lanes, lanes)]
                    high = value.astype(jnp.bfloat16).astype(jnp.float32)
                    rest = value - high
                    middle = rest.astype(jnp.bfloat16).astype(jnp.float32)
                    low = rest - middle
                    other_high, other_middle, other_low = roll(high), roll(middle), roll(low)
                    rows = [
                        [jnp.where(left, high, other_middle), jnp.where(left, low, other_high)],
                        [jnp.where(left, other_high, middle), jnp.where(left, other_low, high)],
                    ]
                    row_at = pl.multiple_of((at // lanes + inner) * lanes, lanes)
                    for half in range(2):
                        spread_ref[slot, pl.ds(row_at + half * edge, edge), :] = jnp.concatenate(
                            rows[half], axis=1
                        ).astype(jnp.bfloat16)
                    parts.append([item.astype(jnp.bfloat16) for item in (high, middle, low)])
                high, middle, low = [jnp.concatenate(item, axis=1) for item in zip(*parts)]
                here = pl.ds(at, turn)
                turned_ref[slot, here, : 2 * edge] = jnp.concatenate([high, middle], axis=0).T
                turned_ref[slot, here, 2 * edge :] = jnp.concatenate([low, high], axis=0).T

    kind = shaped(slots, pairs, 4 * edge, dtype=jnp.bfloat16)
    return kernel_call(body, [kind, kind], [blocks], after=after)


def dot32(left, right):
    return jnp.dot(left, right, preferred_element_type=jnp.float32)


def times(rows, matrix):
    rank = matrix.shape[1]
    high, middle, least = split3(matrix)
    left_high, left_middle, left_least = split3(rows)
    one = jnp.concatenate([high, middle], axis=1)
    wide = dot32(
        jnp.concatenate([left_high, left_middle], axis=1), jnp.concatenate([one, one], axis=0)
    )
    thin = dot32(
        jnp.concatenate([left_least, left_high], axis=1), jnp.concatenate([high, least], axis=0)
    )
    return (thin + wide[:, rank:]) + wide[:, :rank]


def stack_parts(matrix):
    high, middle, least = split3(matrix)
    none = jnp.zeros_like(high)
    return jnp.concatenate(
        [
            jnp.concatenate([high, high, high, none], axis=0),
            jnp.concatenate([middle, middle, none, least], axis=0),
        ],
        axis=1,
    )


def gram_parts(rows):
    rank = rows.shape[1]
    high, middle, least = split3(rows)
    both = jnp.concatenate([high, middle], axis=1)
    turned = both.T
    return dot32(turned, both), dot32(turned[:rank], least)


def join_gram(parts):
    square, rest = parts
    rank = rest.shape[0]
    rest = rest + square[:rank, rank:]
    return (square[rank:, rank:] + (rest + rest.T)) + square[:rank, :rank]


def split3(value):
    high = value.astype(jnp.bfloat16)
    rest = value - high.astype(jnp.float32)
    middle = rest.astype(jnp.bfloat16)
    low = (rest - middle.astype(jnp.float32)).astype(jnp.bfloat16)
    return high, middle, low


def second_mode(terms, inverse, spread_blocks, rows, wide_size):
    low = len(terms)
    pairs, edge, rank = rows.shape
    slots = pairs // 2
    slice_rows = edge // wide_size
    chunk = 4

    def tag_of(ref, d, slot, at):
        return ref[d, slots * edge + slot : slots * edge + slot + 1, at : at + 1]

    def body(*refs):
        term_refs = refs[: len(terms)]
        inverse_ref, spread_ref, rows_ref = refs[len(terms) : len(terms) + 3]
        out_refs = refs[len(terms) + 3 : len(terms) + 3 + low]
        held_ref = refs[-1]
        sums = []
        for slot in range(slots):
            total = None
            for m in range(wide_size):
                for other in range(slots):
                    there = tag_of(term_refs[m % low], m // low, other, 0)
                    same = (there == tag_of(term_refs[0], 0, slot, 0)).astype(jnp.float32)
                    here = slice(other * edge, (other + 1) * edge)
                    part = term_refs[m % low][m // low, here, :] * same
                    total = part if total is None else total + part
            sums.append(total)
        aux = times(jnp.concatenate(sums, axis=0), inverse_ref[...])
        for slot in range(slots):
            weight = tag_of(term_refs[0], 0, slot, live_at)
            stacked = stack_parts(aux[slot * edge : (slot + 1) * edge] * weight)
            rows_i, rows_j = rows_ref[2 * slot], rows_ref[2 * slot + 1]

            def step(index, total_j):
                at = pl.multiple_of(index * (chunk * edge), chunk * edge)
                spread = jnp.dot(
                    spread_ref[slot, pl.ds(at, chunk * edge), :],
                    stacked,
                    preferred_element_type=jnp.float32,
                )
                spread = spread[:, :rank] + spread[:, rank:]
                for inner in range(chunk):
                    part = spread[inner * edge : (inner + 1) * edge]
                    here = index * chunk + inner
                    held_ref[2 * slot, pl.ds(here, 1), :] = jnp.sum(
                        part * rows_j, axis=0, keepdims=True
                    )
                    total_j = total_j + part * rows_ref[2 * slot, pl.ds(here, 1), :]
                return total_j

            held_ref[2 * slot + 1] = lax.fori_loop(
                0, edge // chunk, step, jnp.zeros((edge, rank), jnp.float32), unroll=True
            )
        wide_at = lax.axis_index("wide")
        for place in range(wide_size):
            source = (wide_at ^ place) * slice_rows
            for pair in range(2 * slots):
                out_refs[place % low][place // low, pair] = held_ref[
                    pair, pl.ds(pl.multiple_of(source, slice_rows), slice_rows), :
                ]

    return kernel_call(
        body,
        [shaped(wide_size // low, 2 * slots, slice_rows, rank)] * low,
        list(terms) + [inverse, spread_blocks, rows],
        scratch=[pltpu.VMEM((2 * slots, edge, rank), jnp.float32)],
        about_us=2.5,
    )


def read_coords(terms, slots, edge, axes):
    low = len(terms)
    partners = terms[0].shape[0]

    def body(*refs):
        for j in range(low):
            for d in range(partners):
                tags = refs[j][d, slots * edge : slots * (edge + 1), :axes]
                refs[-1][d * low + j] = tags.astype(jnp.int32)

    return kernel_call(
        body, [shaped(partners * low, slots, axes, dtype=jnp.int32)], list(terms)
    )[0]


def column_gram(coords, terms, inverse, edge, after):
    low = len(terms)
    devices, slots, _ = coords.shape
    rank = inverse.shape[0]
    count = devices * slots

    def body(coord_ref, *refs):
        term_refs = refs[:low]
        inverse_ref, gram_ref, aux_ref = refs[low:]
        wide_at = lax.axis_index("wide")
        aux_ref[...] = jnp.zeros_like(aux_ref)
        blocks_at = [
            coord_ref[wide_at ^ (index // slots), index % slots, 0] for index in range(count)
        ]
        for index in range(count):
            to = jnp.int32(index)
            for earlier in reversed(range(index)):
                to = jnp.where(blocks_at[earlier] == blocks_at[index], earlier, to)
            here = slice(index % slots * edge, (index % slots + 1) * edge)
            place = wide_at ^ (index // slots)
            term = term_refs[0][place // low, here, :]
            for j in range(1, low):
                term = jnp.where(place % low == j, term_refs[j][place // low, here, :], term)
            aux_ref[to] += term
        aux = times(aux_ref[...].reshape(count * edge, rank), inverse_ref[...])
        aux_ref[...] = aux.reshape(count, edge, rank)
        gram_ref[...] = join_gram(gram_parts(aux))

    return kernel_call(
        body,
        [shaped(rank, rank), shaped(count, edge, rank)],
        [coords] + list(terms) + [inverse],
        scalars=1,
        about_us=0.1,
        after=after,
    )


def own_aux(coords, aux, own_rows, after):
    devices, slots, _ = coords.shape
    count, edge, rank = aux.shape
    grain = min(own_rows, edge)
    per_block = edge // grain
    per_device = own_rows // grain

    def body(coord_ref, aux_ref, out_ref, done_ref):
        done_ref[...] = jnp.zeros_like(done_ref)
        out_ref[...] = jnp.zeros_like(out_ref)
        wide_at = lax.axis_index("wide")
        blocks_at = [
            coord_ref[wide_at ^ (index // slots), index % slots, 0] for index in range(count)
        ]
        for index in range(count):
            first = jnp.bool_(True)
            for earlier in range(index):
                first = first & (blocks_at[earlier] != blocks_at[index])
            for part in range(per_block):
                grain_at = blocks_at[index] * per_block + part

                @pl.when(first & (grain_at // per_device == wide_at))
                def _():
                    out_ref[grain_at % per_device] = aux_ref[
                        index, part * grain : (part + 1) * grain, :
                    ]

    owned, done = kernel_call(
        body,
        [shaped(per_device, grain, rank), shaped(8, rank)],
        [coords, aux],
        scalars=1,
        about_us=0.1,
        after=after,
    )
    return owned.reshape(own_rows, rank), done


def pack_pieces(groups, after):
    low = len(groups)
    partners = groups[0].shape[0]

    def body(*refs):
        for d in range(partners):
            for j in range(low):
                refs[low + d][j] = refs[j][d]

    return kernel_call(
        body, [shaped(low, *groups[0].shape[1:])] * partners, list(groups), after=after
    )


def pack_whole(items, after=(), rows=None):
    rows = rows or items[0].shape[0]
    kind = shaped(len(items), rows, *items[0].shape[1:], dtype=items[0].dtype)

    def body(*refs):
        for index, ref in enumerate(refs[:-1]):
            refs[-1][index] = ref[:rows]

    return kernel_call(body, [kind], list(items), after=after)[0]


def with_partners(value, low):
    return [value] + [swap_with(value, "wide", j) for j in range(1, low)]


def plan_sums(coords, rows, narrow_size, own_blocks, after):
    devices, slots, _ = coords.shape
    count = devices * slots * 2
    lanes = min(count * rows, 128)

    def body(coord_ref, out_ref, held_ref):
        narrow_at = lax.axis_index("narrow")
        held_ref[...] = jnp.zeros_like(held_ref)
        ahead = lax.broadcasted_iota(jnp.int32, (rows, lanes), 1) - lax.broadcasted_iota(
            jnp.int32, (rows, lanes), 0
        )
        for index in range(count):
            pair = index % (2 * slots)
            block = coord_ref[index // (2 * slots), pair // 2, 1 + pair % 2]
            to = ((block // own_blocks) ^ narrow_at) * own_blocks + block % own_blocks
            at = index * rows // lanes * lanes
            held_ref[to, :, at : at + lanes] += (ahead == index * rows - at).astype(jnp.float32)
        out_ref[...] = held_ref[...].reshape(out_ref.shape).astype(jnp.bfloat16)

    total = narrow_size * own_blocks
    return kernel_call(
        body,
        [shaped(total * rows, count * rows, dtype=jnp.bfloat16)],
        [coords],
        scalars=1,
        scratch=[pltpu.VMEM((total, rows, count * rows), jnp.float32)],
        after=after,
    )[0]


def add_pieces(plan, pieces, narrow_size, after):
    low, pairs, rows, rank = pieces[0].shape
    part_rows = plan.shape[0] // narrow_size

    def body(plan_ref, *refs):
        terms = jnp.concatenate(
            [ref[...].reshape(low * pairs * rows, rank) for ref in refs[: len(pieces)]], axis=0
        )
        high, middle, least = split3(terms)
        wide = dot32(plan_ref[...], jnp.concatenate([high, middle], axis=1))
        sums = (dot32(plan_ref[...], least) + wide[:, rank:]) + wide[:, :rank]
        for m, out_ref in enumerate(refs[len(pieces) :]):
            out_ref[...] = sums[m * part_rows : (m + 1) * part_rows]

    return kernel_call(
        body, [shaped(part_rows, rank)] * narrow_size, [plan] + list(pieces), after=after
    )


def add_parts(parts, after=(), rows=None):
    count, rank = parts[0].shape
    rows = rows or count

    def body(*refs):
        refs[-1][...] = add_tree([ref[count - rows :, :] for ref in refs[:-1]])

    return kernel_call(body, [shaped(rows, rank)], list(parts), after=after)[0]


def solve_rows(parts, inverse, own_blocks):
    low = len(parts)
    partners, part_rows, rank = parts[0].shape
    rows = part_rows // own_blocks

    def body(*refs):
        wide_at = lax.axis_index("wide")
        for j in range(low):
            solved = times(refs[j][...].reshape(partners * part_rows, rank), refs[low][...])
            for d in range(partners):
                place = wide_at ^ (d * low + j)
                for block in range(own_blocks):
                    at = d * part_rows + block * rows
                    refs[-1][block, place] = solved[at : at + rows]

    return kernel_call(
        body, [shaped(own_blocks, partners * low, rows, rank)], list(parts) + [inverse]
    )[0]


def on_device(blocks, block_coords, block_count, orbital_factor):
    slots, edge = blocks.shape[2:4]
    rank = orbital_factor.shape[1]
    wide_size = lax.axis_size("wide")
    narrow_size = lax.axis_size("narrow")
    low = digits_of(wide_size)[0][1]
    slice_rows = edge // wide_size
    own_blocks = orbital_factor.shape[0] // edge
    own_rows = NP // narrow_size // wide_size

    by_slice = orbital_factor.reshape(own_blocks, wide_size // low, low, slice_rows, rank)
    chip_at = lax.axis_index("wide") // low
    chip_slice = lax.dynamic_index_in_dim(by_slice, chip_at, 1, keepdims=False)
    own_slice = own_part(chip_slice)
    pairs = [send_by_core(chip_slice, [m, m + 1]) for m in range(1, narrow_size - 1, low)]
    single = swap_with(own_slice, "narrow", narrow_size - 1)
    arrived = gather_from(block_coords[0, 0], "wide", skip=1)[1:]
    blocks = stage(blocks[0, 0], [own_slice])
    mine = pack_slices(pairs, single, arrived + [blocks])
    theirs = swap_with(mine, "wide", 1)
    tags, coords = open_tags(block_coords[0, 0], block_count, rank, [mine])
    coords = pack_whole([coords] + arrived)
    wanted = pick_pieces(coords, chip_slice, mine, theirs, narrow_size, [])
    pieces = exchange(wanted, "wide", skip=1)

    spread, turned = split_blocks(blocks, wanted[:1])
    half = add_parts(pieces, [turned], rows=rank // low)
    rows, terms = first_mode(tags, pieces, spread, wide_size, low, [half])
    other_half = swap_with(half, "wide", 1)
    terms = add_parts([terms], [other_half])
    *started, gram_b = start_inverse([half, other_half], None, 1.0, [terms])
    terms = pack_whole(gather_from(terms, "wide", skip=1), after=started[:1])
    inverse_b = end_inverse(*started, [terms])
    column_terms = with_partners(terms, low)
    all_coords = read_coords(column_terms, slots, edge, block_coords.shape[3])

    groups = second_mode(column_terms, inverse_b, turned, rows, wide_size)
    plan = plan_sums(all_coords, slice_rows, narrow_size, own_blocks, groups[:1])
    groups = [groups[0]] + [swap_with(groups[j], "wide", j) for j in range(1, low)]
    packed = pack_pieces(groups, [plan])
    pieces = exchange(packed, "wide", skip=1)

    gram, aux = column_gram(all_coords, column_terms, inverse_b, edge, packed[:1])

    sums = add_pieces(plan, pieces, narrow_size, [gram])
    parts = exchange(sums, "narrow")
    step = narrow_size // 2
    while step > 1:
        gram = add_parts([gram, swap_with(gram, "narrow", step)], sums[:1])
        step //= 2
    aux_owned, done = own_aux(all_coords, aux, own_rows, [gram])
    total = add_parts(parts, [gram, done])
    grams = [gram, swap_with(gram, "narrow", step)]
    started = start_inverse(grams, gram_b, 2.0, [total])
    totals = pack_whole(gather_from(total, "wide", skip=1), after=started[:1])
    inverse_a = end_inverse(*started, [totals])
    orbital_new = solve_rows(with_partners(totals, low), inverse_a, own_blocks)
    return (aux_owned[None], orbital_new.reshape(own_blocks * edge, rank))


def solution(mesh):
    return jax.shard_map(
        on_device,
        mesh=mesh,
        in_specs=(
            P("wide", "narrow", None, None, None),
            P("wide", "narrow", None, None),
            P("wide", "narrow"),
            P("narrow", None),
        ),
        out_specs=(P("narrow", "wide", None), P("narrow", None)),
        check_vma=False,
    )
```

```python
import functools

import jax
import jax.numpy as jnp
from jax import lax
from jax.experimental import pallas as pl
from jax.experimental.pallas import tpu as pltpu
from jax.sharding import PartitionSpec as P

NP = 16384


precise_level = lax.Precision.HIGHEST
in_vmem = pl.BlockSpec(memory_space=pltpu.VMEM)
in_smem = pl.BlockSpec(memory_space=pltpu.SMEM)
live_at = 3
in_hbm = pl.BlockSpec(memory_space=pltpu.HBM)


def product(left, right):
    return jnp.dot(left, right, precision=precise_level, preferred_element_type=jnp.float32)


def kernel_call(body, outputs, operands, scalars=0, scratch=(), about_us=0.3, after=(), far=False):
    after = list(after)

    def whole(*refs):
        body(*refs[: len(operands)], *refs[len(operands) + len(after) :])

    return pl.pallas_call(
        whole,
        out_shape=outputs,
        in_specs=[in_smem] * scalars
        + [in_hbm if far else in_vmem] * (len(operands) - scalars)
        + [pl.BlockSpec(memory_space=pl.ANY)] * len(after),
        out_specs=[in_vmem] * len(outputs),
        scratch_shapes=list(scratch),
        compiler_params=pltpu.CompilerParams(vmem_limit_bytes=24 * 1024 * 1024),
        cost_estimate=pl.CostEstimate(
            flops=int(about_us * 1e6), bytes_accessed=0, transcendentals=0
        ),
    )(*operands, *after)


def shaped(*shape, dtype=jnp.float32):
    return jax.ShapeDtypeStruct(shape, dtype)


def add_tree(items):
    while len(items) > 1:
        items = [items[t] + items[t + 1] for t in range(0, len(items), 2)]
    return items[0]


def digits_of(size):
    digits = []
    stride = 1
    while stride < size:
        left = size // stride
        radix = 2 if left.bit_length() % 2 == 0 else 4
        digits.append((stride, radix))
        stride *= radix
    return digits


def swap_with(value, axis, mask):
    size = lax.axis_size(axis)
    return lax.ppermute(value, axis, [(index, index ^ mask) for index in range(size)])


def send_by_core(value, masks):
    wide_size, narrow_size = lax.axis_size("wide"), lax.axis_size("narrow")
    pairs = [
        (w * narrow_size + n, w * narrow_size + (n ^ masks[w % len(masks)]))
        for w in range(wide_size)
        for n in range(narrow_size)
    ]
    return lax.ppermute(value, ("wide", "narrow"), pairs)


def gather_from(value, axis, skip=0):
    digits = digits_of(lax.axis_size(axis))
    held = {0: value}
    for stride, radix in reversed(digits[skip:]):
        fresh = {}
        for digit in reversed(range(1, radix)):
            for key, item in held.items():
                fresh[key + digit * stride] = swap_with(item, axis, digit * stride)
        held.update(fresh)
    return [held[key] for key in sorted(held)]


def exchange(items, axis, skip=0):
    digits = digits_of(lax.axis_size(axis))
    unit = digits[skip][0] if skip < len(digits) else 1
    items = list(items)
    for stride, radix in digits[skip:]:
        step = stride // unit
        for digit in reversed(range(1, radix)):
            at = [key for key in range(len(items)) if key // step % radix == digit]
            if len(at) == 1:
                items[at[0]] = swap_with(items[at[0]], axis, digit * stride)
            else:
                packed = swap_with(jnp.stack([items[key] for key in at]), axis, digit * stride)
                for place, key in enumerate(at):
                    items[key] = packed[place]
    return items


def eliminate(held, left_ref, right_ref, blocks):
    step, size = held[0].shape
    sub = lax.broadcasted_iota(jnp.int32, (step, size), 0)
    lane = lax.broadcasted_iota(jnp.int32, (step, size), 1)

    def splat_lane(value, index):
        return jnp.broadcast_to(value[:, index : index + 1], (step, size))

    def splat_row(value, index):
        return jnp.broadcast_to(value[index : index + 1, :], (step, size))

    for block in blocks:
        at = slice(step * block, step * block + step)
        inside = (lane >= step * block) & (lane < step * block + step)
        upto = lane < step * block + step
        unit = (lane - step * block == sub).astype(jnp.float32)
        pivots = [splat_lane(held[block], step * block + t) for t in range(step)]
        panel = jnp.where(inside, unit, held[block])
        left_ref[at, :] = jnp.where(upto, panel, 0.0)
        for p in range(0, step, 2):
            first, second = sub == p, sub == p + 1
            corner = splat_row(pivots[p], p)
            above, below = splat_row(pivots[p + 1], p), splat_row(pivots[p], p + 1)
            last = splat_row(pivots[p + 1], p + 1)
            scaled = 1.0 / (corner * last - above * below)
            i11, i12, i21, i22 = last * scaled, -above * scaled, -below * scaled, corner * scaled
            one = jnp.where(
                first, -i11, jnp.where(second, -i21, pivots[p] * i11 + pivots[p + 1] * i21)
            )
            two = jnp.where(
                first, -i12, jnp.where(second, -i22, pivots[p] * i12 + pivots[p + 1] * i22)
            )

            def clear(value):
                kept = jnp.where(first | second, 0.0, value)
                return kept - (one * splat_row(value, p) + two * splat_row(value, p + 1))

            for t in range(p + 2, step):
                pivots[t] = clear(pivots[t])
            panel = clear(panel)
        right_ref[at, :] = jnp.where(upto, panel, 0.0)
        rows = [splat_row(panel, t) for t in range(step)]
        for index in range(block + 1, len(held)):
            pairs = [splat_lane(held[index], step * block + t) * rows[t] for t in range(step)]
            held[index] = jnp.where(inside, 0.0, held[index]) - add_tree(pairs)
    return held


pivot_rows = 16


def first_steps(count):
    return count * 3 // 4


def start_inverse(grams, other, scale, after):
    size = grams[0].shape[-1]
    step = pivot_rows
    count = size // step
    own = other is None
    operands = list(grams) + ([] if own else [other])

    def body(*refs):
        parts, refs = refs[: len(grams)], refs[len(grams) :]
        held = []
        for block in range(count):
            at = slice(step * block, step * block + step)
            if own:
                half = size // 2
                here = slice(step * block % half, step * block % half + step)
                core = lax.axis_index("wide") % 2
                total = jnp.where(
                    core == step * block // half, parts[0][here, :], parts[1][here, :]
                )
                refs[3][at, :] = total
                held.append(total * total)
            else:
                total = add_tree([part[at, :] for part in parts])
                held.append(scale * total * refs[0][at, :])
        held_ref, left_ref, right_ref = refs[:3] if own else refs[1:]
        held = eliminate(held, left_ref, right_ref, range(first_steps(count)))
        for block in range(count):
            at = slice(step * block, step * block + step)
            held_ref[at, :] = held[block]
            if block >= first_steps(count):
                left_ref[at, :] = jnp.zeros_like(held[block])
                right_ref[at, :] = jnp.zeros_like(held[block])

    outputs = [shaped(size, size)] * (4 if own else 3)
    return kernel_call(body, outputs, operands, about_us=1.8, after=after)


def end_inverse(held, left, right, after):
    size = held.shape[0]
    step = pivot_rows
    count = size // step

    def body(held_ref, left_in, right_in, out_ref, left_ref, right_ref):
        done = first_steps(count) * step
        left_ref[:done, :] = left_in[:done, :]
        right_ref[:done, :] = right_in[:done, :]
        rows = [held_ref[step * block : step * block + step, :] for block in range(count)]
        eliminate(rows, left_ref, right_ref, range(first_steps(count), count))
        out_ref[...] = lax.dot_general(
            left_ref[...],
            right_ref[...],
            (((0,), (0,)), ((), ())),
            precision=precise_level,
            preferred_element_type=jnp.float32,
        )

    return kernel_call(
        body,
        [shaped(size, size)],
        [held, left, right],
        scratch=[pltpu.VMEM((size, size), jnp.float32)] * 2,
        about_us=1.6,
        after=after,
    )[0]


def own_part(chip_slice):
    own_blocks, low, rows, rank = chip_slice.shape

    def body(in_ref, out_ref):
        core = lax.axis_index("wide") % low
        for block in range(own_blocks):
            out_ref[block] = in_ref[block, core]

    return kernel_call(body, [shaped(own_blocks, rows, rank)], [chip_slice])[0]


def open_tags(coords, count, rank, after):
    slots, axes = coords.shape

    def body(coords_ref, count_ref, tag_ref, out_ref):
        slot_at = lax.broadcasted_iota(jnp.int32, (slots, 1), 0)
        tag_ref[...] = jnp.zeros_like(tag_ref)
        tag_ref[:slots, :axes] = coords_ref[...].astype(jnp.float32)
        tag_ref[:slots, axes : axes + 1] = (slot_at < count_ref[...]).astype(jnp.float32)
        out_ref[...] = coords_ref[...]

    return kernel_call(
        body,
        [shaped(8, rank), shaped(slots, axes, dtype=jnp.int32)],
        [coords, count],
        after=after,
    )


def stage(value, after):
    def body(in_ref, out_ref, sem):
        copy = pltpu.make_async_copy(in_ref, out_ref, sem)
        copy.start()
        copy.wait()

    return kernel_call(
        body,
        [shaped(*value.shape)],
        [value],
        scratch=[pltpu.SemaphoreType.DMA],
        after=after,
        far=True,
    )[0]


def pack_slices(pairs, single, after):
    own_blocks, low, rows, rank = pairs[0].shape if pairs else (single.shape[0], 0, 0, 0)
    _, rows, rank = single.shape
    total = own_blocks * (low * len(pairs) + 1)

    def body(*refs):
        out_ref = refs[-1]
        for index, ref in enumerate(refs[: len(pairs)]):
            at = index * own_blocks * low
            out_ref[at : at + own_blocks * low] = ref[...].reshape(own_blocks * low, rows, rank)
        out_ref[total - own_blocks :] = refs[len(pairs)][...]

    return kernel_call(
        body, [shaped(total, rows, rank)], list(pairs) + [single], after=after
    )[0]


def gram_of(items):
    rank = items[0].shape[-1]

    def body(*refs):
        rows = jnp.concatenate([ref[...].reshape(-1, rank) for ref in refs[:-1]], axis=0)
        refs[-1][...] = join_gram(gram_parts(rows))

    return kernel_call(body, [shaped(rank, rank)], list(items))[0]


def pick_pieces(coords, own, mine, theirs, gram, narrow_size):
    own_blocks, low, rows, rank = own.shape
    partners, slots, _ = coords.shape
    piece_rows = slots * 2 * low * rows
    share = rank // low

    def body(there_ref, own_ref, mine_ref, theirs_ref, gram_here, *refs):
        out_refs, (coord_ref, gram_ref, all_ref, sem) = refs[:partners], refs[partners:]
        narrow_at = lax.axis_index("narrow")
        core = lax.axis_index("wide") % low
        copy = pltpu.make_async_copy(there_ref, coord_ref, sem)
        copy.start()
        gram_ref[...] = gram_here[...] + join_gram(gram_parts(theirs_ref[...].reshape(-1, rank)))
        for out_ref in out_refs:
            out_ref[piece_rows:, :] = gram_ref[pl.ds(pl.multiple_of(core * share, share), share), :]
        for j in range(low):
            for local in range(own_blocks):
                all_ref[j * own_blocks + local] = own_ref[local, j]
                for m in range(1, narrow_size):
                    last = m == narrow_size - 1
                    holder = j if last else (m - 1) % low
                    at = (m - 1) // low * own_blocks * low + local * low + j
                    if last:
                        at = (narrow_size - 2) * own_blocks + local
                    all_ref[(m * low + j) * own_blocks + local] = jnp.where(
                        core == holder, mine_ref[at], theirs_ref[at]
                    )
        copy.wait()
        for d, out_ref in enumerate(out_refs):
            for pair in range(slots * 2):
                block = coord_ref[d, pair // 2, 1 + pair % 2]
                owner = (block // own_blocks) ^ narrow_at
                for j in range(low):
                    at = (owner * low + (core ^ j)) * own_blocks + block % own_blocks
                    to = (pair * low + j) * rows
                    out_ref[to : to + rows, :] = all_ref[at]

    return kernel_call(
        body,
        [shaped(piece_rows + share, rank)] * partners,
        [coords, own, mine, theirs, gram],
        scratch=[
            pltpu.SMEM(coords.shape, jnp.int32),
            pltpu.VMEM((rank, rank), jnp.float32),
            pltpu.VMEM((narrow_size * low * own_blocks, rows, rank), jnp.float32),
            pltpu.SemaphoreType.DMA,
        ],
    )


def first_mode(tags, pieces, spread, wide_size, low, after):
    rank = pieces[0].shape[1]
    slots, _, width = spread.shape
    edge = width // 4
    pairs = 2 * slots
    slice_rows = edge // wide_size
    chunk = 4

    def body(tag_ref, *refs):
        piece_refs = refs[: len(pieces)]
        spread_ref, rows_ref, term_ref, held_ref = refs[len(pieces) :]
        term_ref[slots * edge :, :] = tag_ref[...]
        wide_at = lax.axis_index("wide")
        for d, piece_ref in enumerate(piece_refs):
            for j in range(low):
                place = wide_at ^ (d * low + j)
                for pair in range(pairs):
                    at = (pair * low + j) * slice_rows
                    held_ref[pair, place] = piece_ref[at : at + slice_rows, :]
        rows_ref[...] = held_ref[...].reshape(pairs, edge, rank)
        for slot in range(slots):
            stacked = stack_parts(rows_ref[2 * slot + 1])

            def step(index, total):
                at = pl.multiple_of(index * (chunk * edge), chunk * edge)
                product = dot32(spread_ref[slot, pl.ds(at, chunk * edge), :], stacked)
                product = product[:, :rank] + product[:, rank:]
                for inner in range(chunk):
                    row = rows_ref[2 * slot, pl.ds(index * chunk + inner, 1), :]
                    total = total + product[inner * edge : (inner + 1) * edge] * row
                return total

            total = lax.fori_loop(
                0, edge // chunk, step, jnp.zeros((edge, rank), jnp.float32), unroll=True
            )
            live = tag_ref[slot : slot + 1, live_at : live_at + 1]
            term_ref[slot * edge : (slot + 1) * edge, :] = total * live

    return kernel_call(
        body,
        [shaped(pairs, edge, rank), shaped(slots * edge + tags.shape[0], rank)],
        [tags] + list(pieces) + [spread],
        scratch=[pltpu.VMEM((pairs, wide_size, slice_rows, rank), jnp.float32)],
        about_us=3.0,
        after=after,
    )


def split_blocks(blocks, after):
    slots, edge, pairs = blocks.shape
    turn = 512
    lanes = 2 * edge

    def body(in_ref, spread_ref, turned_ref):
        left = lax.broadcasted_iota(jnp.int32, (edge, lanes), 1) < edge

        def roll(value):
            return pltpu.roll(value, edge, 1)

        for slot in range(slots):

            @pl.loop(0, pairs // turn)
            def _(index):
                at = pl.multiple_of(index * turn, turn)
                parts = []
                for inner in range(turn // lanes):
                    value = in_ref[slot, :, pl.ds(at + inner * lanes, lanes)]
                    high = value.astype(jnp.bfloat16).astype(jnp.float32)
                    rest = value - high
                    middle = rest.astype(jnp.bfloat16).astype(jnp.float32)
                    low = rest - middle
                    first = roll(jnp.where(left, middle, high))
                    second = roll(jnp.where(left, high, low))
                    rows = [
                        [jnp.where(left, high, first), jnp.where(left, low, second)],
                        [jnp.where(left, first, middle), jnp.where(left, second, high)],
                    ]
                    row_at = pl.multiple_of((at // lanes + inner) * lanes, lanes)
                    for half in range(2):
                        spread_ref[slot, pl.ds(row_at + half * edge, edge), :] = jnp.concatenate(
                            rows[half], axis=1
                        ).astype(jnp.bfloat16)
                    parts.append([item.astype(jnp.bfloat16) for item in (high, middle, low)])
                high, middle, low = [jnp.concatenate(item, axis=1) for item in zip(*parts)]
                here = pl.ds(at, turn)
                turned_ref[slot, here, : 2 * edge] = jnp.concatenate([high, middle], axis=0).T
                turned_ref[slot, here, 2 * edge :] = jnp.concatenate([low, high], axis=0).T

    kind = shaped(slots, pairs, 4 * edge, dtype=jnp.bfloat16)
    return kernel_call(body, [kind, kind], [blocks], after=after)


def dot32(left, right):
    return jnp.dot(left, right, preferred_element_type=jnp.float32)


def times(rows, matrix):
    rank = matrix.shape[1]
    high, middle, least = split3(matrix)
    left_high, left_middle, left_least = split3(rows)
    one = jnp.concatenate([high, middle], axis=1)
    wide = dot32(
        jnp.concatenate([left_high, left_middle], axis=1), jnp.concatenate([one, one], axis=0)
    )
    thin = dot32(
        jnp.concatenate([left_least, left_high], axis=1), jnp.concatenate([high, least], axis=0)
    )
    return (thin + wide[:, rank:]) + wide[:, :rank]


def stack_parts(matrix):
    high, middle, least = split3(matrix)
    none = jnp.zeros_like(high)
    return jnp.concatenate(
        [
            jnp.concatenate([high, high, high, none], axis=0),
            jnp.concatenate([middle, middle, none, least], axis=0),
        ],
        axis=1,
    )


def gram_parts(rows):
    rank = rows.shape[1]
    high, middle, least = split3(rows)
    both = jnp.concatenate([high, middle], axis=1)
    turned = both.T
    return dot32(turned, both), dot32(turned[:rank], least)


def join_gram(parts):
    square, rest = parts
    rank = rest.shape[0]
    rest = rest + square[:rank, rank:]
    return (square[rank:, rank:] + (rest + rest.T)) + square[:rank, :rank]


def split3(value):
    high = value.astype(jnp.bfloat16)
    rest = value - high.astype(jnp.float32)
    middle = rest.astype(jnp.bfloat16)
    low = (rest - middle.astype(jnp.float32)).astype(jnp.bfloat16)
    return high, middle, low


def tag_of(ref, d, slots, edge, slot, at):
    return ref[d, slots * edge + slot : slots * edge + slot + 1, at : at + 1]


def sum_terms(terms, own, slots, edge, after):
    partners, _, rank = terms.shape

    def body(term_ref, own_ref, out_ref):
        for slot in range(slots):
            here = tag_of(own_ref, 0, slots, edge, slot, 0)
            total = None
            for d in range(partners):
                for other in range(slots):
                    same = (tag_of(term_ref, d, slots, edge, other, 0) == here).astype(jnp.float32)
                    part = term_ref[d, other * edge : (other + 1) * edge, :] * same
                    total = part if total is None else total + part
            out_ref[slot * edge : (slot + 1) * edge, :] = total

    return kernel_call(body, [shaped(slots * edge, rank)], [terms, own], after=after)[0]


def second_mode(partial, terms, inverse, spread_blocks, rows, wide_size):
    low = len(terms)
    pairs, edge, rank = rows.shape
    slots = pairs // 2
    slice_rows = edge // wide_size
    chunk = 4

    def body(partial_ref, *refs):
        term_refs = refs[: len(terms)]
        inverse_ref, spread_ref, rows_ref = refs[len(terms) : len(terms) + 3]
        out_refs = refs[len(terms) + 3 : len(terms) + 3 + low]
        held_ref = refs[-1]
        sums = []
        for slot in range(slots):
            total = partial_ref[slot * edge : (slot + 1) * edge, :]
            here = tag_of(term_refs[0], 0, slots, edge, slot, 0)
            for m in range(wide_size):
                if m % low == 0:
                    continue
                for other in range(slots):
                    there = tag_of(term_refs[m % low], m // low, slots, edge, other, 0)
                    same = (there == here).astype(jnp.float32)
                    part = term_refs[m % low][m // low, other * edge : (other + 1) * edge, :]
                    total = total + part * same
            sums.append(total)
        aux = times(jnp.concatenate(sums, axis=0), inverse_ref[...])
        for slot in range(slots):
            weight = tag_of(term_refs[0], 0, slots, edge, slot, live_at)
            stacked = stack_parts(aux[slot * edge : (slot + 1) * edge] * weight)
            rows_i, rows_j = rows_ref[2 * slot], rows_ref[2 * slot + 1]

            def step(index, total_j):
                at = pl.multiple_of(index * (chunk * edge), chunk * edge)
                spread = jnp.dot(
                    spread_ref[slot, pl.ds(at, chunk * edge), :],
                    stacked,
                    preferred_element_type=jnp.float32,
                )
                spread = spread[:, :rank] + spread[:, rank:]
                for inner in range(chunk):
                    part = spread[inner * edge : (inner + 1) * edge]
                    here = index * chunk + inner
                    held_ref[2 * slot, pl.ds(here, 1), :] = jnp.sum(
                        part * rows_j, axis=0, keepdims=True
                    )
                    total_j = total_j + part * rows_ref[2 * slot, pl.ds(here, 1), :]
                return total_j

            held_ref[2 * slot + 1] = lax.fori_loop(
                0, edge // chunk, step, jnp.zeros((edge, rank), jnp.float32), unroll=True
            )
        wide_at = lax.axis_index("wide")
        for place in range(wide_size):
            source = (wide_at ^ place) * slice_rows
            for pair in range(2 * slots):
                out_refs[place % low][place // low, pair] = held_ref[
                    pair, pl.ds(pl.multiple_of(source, slice_rows), slice_rows), :
                ]

    return kernel_call(
        body,
        [shaped(wide_size // low, 2 * slots, slice_rows, rank)] * low,
        [partial] + list(terms) + [inverse, spread_blocks, rows],
        scratch=[pltpu.VMEM((2 * slots, edge, rank), jnp.float32)],
        about_us=2.5,
    )


def read_coords(terms, slots, edge, axes):
    low = len(terms)
    partners = terms[0].shape[0]

    def body(*refs):
        for j in range(low):
            for d in range(partners):
                tags = refs[j][d, slots * edge : slots * (edge + 1), :axes]
                refs[-1][d * low + j] = tags.astype(jnp.int32)

    return kernel_call(
        body, [shaped(partners * low, slots, axes, dtype=jnp.int32)], list(terms)
    )[0]


def column_gram(coords, terms, inverse, edge, after):
    low = len(terms)
    devices, slots, _ = coords.shape
    rank = inverse.shape[0]
    count = devices * slots

    def body(coord_ref, *refs):
        term_refs = refs[:low]
        inverse_ref, gram_ref, aux_ref = refs[low:]
        wide_at = lax.axis_index("wide")
        aux_ref[...] = jnp.zeros_like(aux_ref)
        blocks_at = [
            coord_ref[wide_at ^ (index // slots), index % slots, 0] for index in range(count)
        ]
        for index in range(count):
            to = jnp.int32(index)
            for earlier in reversed(range(index)):
                to = jnp.where(blocks_at[earlier] == blocks_at[index], earlier, to)
            here = slice(index % slots * edge, (index % slots + 1) * edge)
            place = wide_at ^ (index // slots)
            term = term_refs[0][place // low, here, :]
            for j in range(1, low):
                term = jnp.where(place % low == j, term_refs[j][place // low, here, :], term)
            aux_ref[to] += term
        aux = times(aux_ref[...].reshape(count * edge, rank), inverse_ref[...])
        aux_ref[...] = aux.reshape(count, edge, rank)
        gram_ref[...] = join_gram(gram_parts(aux))

    return kernel_call(
        body,
        [shaped(rank, rank), shaped(count, edge, rank)],
        [coords] + list(terms) + [inverse],
        scalars=1,
        about_us=0.1,
        after=after,
    )


def own_aux(coords, aux, own_rows, after):
    devices, slots, _ = coords.shape
    count, edge, rank = aux.shape
    grain = min(own_rows, edge)
    per_block = edge // grain
    per_device = own_rows // grain

    def body(coord_ref, aux_ref, out_ref, done_ref):
        done_ref[...] = jnp.zeros_like(done_ref)
        out_ref[...] = jnp.zeros_like(out_ref)
        wide_at = lax.axis_index("wide")
        blocks_at = [
            coord_ref[wide_at ^ (index // slots), index % slots, 0] for index in range(count)
        ]
        for index in range(count):
            first = jnp.bool_(True)
            for earlier in range(index):
                first = first & (blocks_at[earlier] != blocks_at[index])
            for part in range(per_block):
                grain_at = blocks_at[index] * per_block + part

                @pl.when(first & (grain_at // per_device == wide_at))
                def _():
                    out_ref[grain_at % per_device] = aux_ref[
                        index, part * grain : (part + 1) * grain, :
                    ]

    owned, done = kernel_call(
        body,
        [shaped(per_device, grain, rank), shaped(8, rank)],
        [coords, aux],
        scalars=1,
        about_us=0.1,
        after=after,
    )
    return owned.reshape(own_rows, rank), done


def pack_pieces(groups, after):
    low = len(groups)
    partners = groups[0].shape[0]

    def body(*refs):
        for d in range(partners):
            for j in range(low):
                refs[low + d][j] = refs[j][d]

    return kernel_call(
        body, [shaped(low, *groups[0].shape[1:])] * partners, list(groups), after=after
    )


def pack_whole(items, after=(), rows=None):
    rows = rows or items[0].shape[0]
    kind = shaped(len(items), rows, *items[0].shape[1:], dtype=items[0].dtype)

    def body(*refs):
        for index, ref in enumerate(refs[:-1]):
            refs[-1][index] = ref[:rows]

    return kernel_call(body, [kind], list(items), after=after)[0]


def with_partners(value, low):
    return [value] + [swap_with(value, "wide", j) for j in range(1, low)]


def plan_sums(coords, rows, narrow_size, own_blocks, after):
    devices, slots, _ = coords.shape
    count = devices * slots * 2
    lanes = min(count * rows, 128)

    def body(coord_ref, out_ref, held_ref):
        narrow_at = lax.axis_index("narrow")
        held_ref[...] = jnp.zeros_like(held_ref)
        ahead = lax.broadcasted_iota(jnp.int32, (rows, lanes), 1) - lax.broadcasted_iota(
            jnp.int32, (rows, lanes), 0
        )
        for index in range(count):
            pair = index % (2 * slots)
            block = coord_ref[index // (2 * slots), pair // 2, 1 + pair % 2]
            to = ((block // own_blocks) ^ narrow_at) * own_blocks + block % own_blocks
            at = index * rows // lanes * lanes
            held_ref[to, :, at : at + lanes] += (ahead == index * rows - at).astype(jnp.float32)
        out_ref[...] = held_ref[...].reshape(out_ref.shape).astype(jnp.bfloat16)

    total = narrow_size * own_blocks
    return kernel_call(
        body,
        [shaped(total * rows, count * rows, dtype=jnp.bfloat16)],
        [coords],
        scalars=1,
        scratch=[pltpu.VMEM((total, rows, count * rows), jnp.float32)],
        after=after,
    )[0]


def add_pieces(plan, pieces, narrow_size, after):
    low, pairs, rows, rank = pieces[0].shape
    part_rows = plan.shape[0] // narrow_size

    def body(plan_ref, *refs):
        terms = jnp.concatenate(
            [ref[...].reshape(low * pairs * rows, rank) for ref in refs[: len(pieces)]], axis=0
        )
        high, middle, least = split3(terms)
        wide = dot32(plan_ref[...], jnp.concatenate([high, middle], axis=1))
        sums = (dot32(plan_ref[...], least) + wide[:, rank:]) + wide[:, :rank]
        for m, out_ref in enumerate(refs[len(pieces) :]):
            out_ref[...] = sums[m * part_rows : (m + 1) * part_rows]

    return kernel_call(
        body, [shaped(part_rows, rank)] * narrow_size, [plan] + list(pieces), after=after
    )


def add_parts(parts, after=(), rows=None):
    count, rank = parts[0].shape
    rows = rows or count

    def body(*refs):
        refs[-1][...] = add_tree([ref[count - rows :, :] for ref in refs[:-1]])

    return kernel_call(body, [shaped(rows, rank)], list(parts), after=after)[0]


def solve_rows(rows, inverse, after):
    shape = rows.shape

    def body(rows_ref, inverse_ref, out_ref):
        solved = times(rows_ref[...].reshape(-1, shape[-1]), inverse_ref[...])
        out_ref[...] = solved.reshape(shape)

    return kernel_call(body, [shaped(*shape)], [rows, inverse], after=after)[0]


def lay_rows(solved, others, inverse, own_blocks):
    low = 1 + len(others)
    partners, part_rows, rank = solved.shape
    rows = part_rows // own_blocks

    def body(solved_ref, *refs):
        wide_at = lax.axis_index("wide")
        inverse_ref, out_ref = refs[len(others) :]
        for j in range(low):
            if j == 0:
                value = solved_ref[...].reshape(partners * part_rows, rank)
            else:
                value = times(
                    refs[j - 1][...].reshape(partners * part_rows, rank), inverse_ref[...]
                )
            for d in range(partners):
                place = wide_at ^ (d * low + j)
                for block in range(own_blocks):
                    at = d * part_rows + block * rows
                    out_ref[block, place] = value[at : at + rows]

    return kernel_call(
        body,
        [shaped(own_blocks, partners * low, rows, rank)],
        [solved] + list(others) + [inverse],
    )[0]


def on_device(blocks, block_coords, block_count, orbital_factor):
    slots, edge = blocks.shape[2:4]
    rank = orbital_factor.shape[1]
    wide_size = lax.axis_size("wide")
    narrow_size = lax.axis_size("narrow")
    low = digits_of(wide_size)[0][1]
    slice_rows = edge // wide_size
    own_blocks = orbital_factor.shape[0] // edge
    own_rows = NP // narrow_size // wide_size

    by_slice = orbital_factor.reshape(own_blocks, wide_size // low, low, slice_rows, rank)
    chip_at = lax.axis_index("wide") // low
    chip_slice = lax.dynamic_index_in_dim(by_slice, chip_at, 1, keepdims=False)
    own_slice = own_part(chip_slice)
    pairs = [send_by_core(chip_slice, [m, m + 1]) for m in range(1, narrow_size - 1, low)]
    single = swap_with(own_slice, "narrow", narrow_size - 1)
    arrived = gather_from(block_coords[0, 0], "wide", skip=1)[1:]
    blocks = stage(blocks[0, 0], [own_slice])
    mine = pack_slices(pairs, single, arrived + [blocks])
    theirs = swap_with(mine, "wide", 1)
    tags, coords = open_tags(block_coords[0, 0], block_count, rank, [mine])
    coords = pack_whole([coords] + arrived)
    gram = gram_of([chip_slice, mine])
    wanted = pick_pieces(coords, chip_slice, mine, theirs, gram, narrow_size)
    pieces = exchange(wanted, "wide", skip=1)

    spread, turned = split_blocks(blocks, wanted[:1])
    half = add_parts(pieces, [turned], rows=rank // low)
    rows, terms = first_mode(tags, pieces, spread, wide_size, low, [half])
    other_half = swap_with(half, "wide", 1)
    terms = add_parts([terms], [other_half])
    *started, gram_b = start_inverse([half, other_half], None, 1.0, [terms])
    terms = pack_whole(gather_from(terms, "wide", skip=1), after=started[:1])
    inverse_b = end_inverse(*started, [terms])
    column_terms = with_partners(terms, low)
    all_coords = read_coords(column_terms, slots, edge, block_coords.shape[3])

    partial = sum_terms(terms, terms, slots, edge, [inverse_b])
    groups = second_mode(partial, column_terms, inverse_b, turned, rows, wide_size)
    plan = plan_sums(all_coords, slice_rows, narrow_size, own_blocks, groups[:1])
    groups = [groups[0]] + [swap_with(groups[j], "wide", j) for j in range(1, low)]
    packed = pack_pieces(groups, [plan])
    pieces = exchange(packed, "wide", skip=1)

    gram, aux = column_gram(all_coords, column_terms, inverse_b, edge, packed[:1])

    sums = add_pieces(plan, pieces, narrow_size, [gram])
    parts = exchange(sums, "narrow")
    step = narrow_size // 2
    while step > 1:
        gram = add_parts([gram, swap_with(gram, "narrow", step)], sums[:1])
        step //= 2
    aux_owned, done = own_aux(all_coords, aux, own_rows, [gram])
    total = add_parts(parts, [gram, done])
    grams = [gram, swap_with(gram, "narrow", step)]
    started = start_inverse(grams, gram_b, 2.0, [total])
    totals = pack_whole(gather_from(total, "wide", skip=1), after=started[:1])
    inverse_a = end_inverse(*started, [totals])
    solved = solve_rows(totals, inverse_a, [])
    orbital_new = lay_rows(solved, with_partners(totals, low)[1:], inverse_a, own_blocks)
    return (aux_owned[None], orbital_new.reshape(own_blocks * edge, rank))


def solution(mesh):
    return jax.shard_map(
        on_device,
        mesh=mesh,
        in_specs=(
            P("wide", "narrow", None, None, None),
            P("wide", "narrow", None, None),
            P("wide", "narrow"),
            P("narrow", None),
        ),
        out_specs=(P("narrow", "wide", None), P("narrow", None)),
        check_vma=False,
    )
```

```python
import functools

import jax
import jax.numpy as jnp
from jax import lax
from jax.experimental import pallas as pl
from jax.experimental.pallas import tpu as pltpu
from jax.sharding import PartitionSpec as P

NP = 16384


precise_level = lax.Precision.HIGHEST
in_vmem = pl.BlockSpec(memory_space=pltpu.VMEM)
in_smem = pl.BlockSpec(memory_space=pltpu.SMEM)
live_at = 3
in_hbm = pl.BlockSpec(memory_space=pltpu.HBM)


def product(left, right):
    return jnp.dot(left, right, precision=precise_level, preferred_element_type=jnp.float32)


def kernel_call(body, outputs, operands, scalars=0, scratch=(), about_us=0.3, after=(), far=False):
    after = list(after)

    def whole(*refs):
        body(*refs[: len(operands)], *refs[len(operands) + len(after) :])

    return pl.pallas_call(
        whole,
        out_shape=outputs,
        in_specs=[in_smem] * scalars
        + [in_hbm if far else in_vmem] * (len(operands) - scalars)
        + [pl.BlockSpec(memory_space=pl.ANY)] * len(after),
        out_specs=[in_vmem] * len(outputs),
        scratch_shapes=list(scratch),
        compiler_params=pltpu.CompilerParams(vmem_limit_bytes=24 * 1024 * 1024),
        cost_estimate=pl.CostEstimate(
            flops=int(about_us * 1e6), bytes_accessed=0, transcendentals=0
        ),
    )(*operands, *after)


def shaped(*shape, dtype=jnp.float32):
    return jax.ShapeDtypeStruct(shape, dtype)


def add_tree(items):
    while len(items) > 1:
        items = [items[t] + items[t + 1] for t in range(0, len(items), 2)]
    return items[0]


def digits_of(size):
    digits = []
    stride = 1
    while stride < size:
        left = size // stride
        radix = 2 if left.bit_length() % 2 == 0 else 4
        digits.append((stride, radix))
        stride *= radix
    return digits


def swap_with(value, axis, mask):
    size = lax.axis_size(axis)
    return lax.ppermute(value, axis, [(index, index ^ mask) for index in range(size)])


def send_by_core(value, masks):
    wide_size, narrow_size = lax.axis_size("wide"), lax.axis_size("narrow")
    pairs = [
        (w * narrow_size + n, w * narrow_size + (n ^ masks[w % len(masks)]))
        for w in range(wide_size)
        for n in range(narrow_size)
    ]
    return lax.ppermute(value, ("wide", "narrow"), pairs)


def gather_from(value, axis, skip=0):
    digits = digits_of(lax.axis_size(axis))
    held = {0: value}
    for stride, radix in reversed(digits[skip:]):
        fresh = {}
        for digit in reversed(range(1, radix)):
            for key, item in held.items():
                fresh[key + digit * stride] = swap_with(item, axis, digit * stride)
        held.update(fresh)
    return [held[key] for key in sorted(held)]


def exchange(items, axis, skip=0):
    digits = digits_of(lax.axis_size(axis))
    unit = digits[skip][0] if skip < len(digits) else 1
    items = list(items)
    for stride, radix in digits[skip:]:
        step = stride // unit
        for digit in reversed(range(1, radix)):
            at = [key for key in range(len(items)) if key // step % radix == digit]
            if len(at) == 1:
                items[at[0]] = swap_with(items[at[0]], axis, digit * stride)
            else:
                packed = swap_with(jnp.stack([items[key] for key in at]), axis, digit * stride)
                for place, key in enumerate(at):
                    items[key] = packed[place]
    return items


def eliminate(held, left_ref, right_ref, blocks):
    step, size = held[0].shape
    sub = lax.broadcasted_iota(jnp.int32, (step, size), 0)
    lane = lax.broadcasted_iota(jnp.int32, (step, size), 1)

    def splat_lane(value, index):
        return jnp.broadcast_to(value[:, index : index + 1], (step, size))

    def splat_row(value, index):
        return jnp.broadcast_to(value[index : index + 1, :], (step, size))

    for block in blocks:
        at = slice(step * block, step * block + step)
        inside = (lane >= step * block) & (lane < step * block + step)
        upto = lane < step * block + step
        unit = (lane - step * block == sub).astype(jnp.float32)
        pivots = [splat_lane(held[block], step * block + t) for t in range(step)]
        panel = jnp.where(inside, unit, held[block])
        left_ref[at, :] = jnp.where(upto, panel, 0.0)
        for p in range(0, step, 2):
            first, second = sub == p, sub == p + 1
            corner = splat_row(pivots[p], p)
            above, below = splat_row(pivots[p + 1], p), splat_row(pivots[p], p + 1)
            last = splat_row(pivots[p + 1], p + 1)
            scaled = 1.0 / (corner * last - above * below)
            i11, i12, i21, i22 = last * scaled, -above * scaled, -below * scaled, corner * scaled
            one = jnp.where(
                first, -i11, jnp.where(second, -i21, pivots[p] * i11 + pivots[p + 1] * i21)
            )
            two = jnp.where(
                first, -i12, jnp.where(second, -i22, pivots[p] * i12 + pivots[p + 1] * i22)
            )

            def clear(value):
                kept = jnp.where(first | second, 0.0, value)
                return kept - (one * splat_row(value, p) + two * splat_row(value, p + 1))

            for t in range(p + 2, step):
                pivots[t] = clear(pivots[t])
            panel = clear(panel)
        right_ref[at, :] = jnp.where(upto, panel, 0.0)
        rows = [splat_row(panel, t) for t in range(step)]
        for index in range(block + 1, len(held)):
            pairs = [splat_lane(held[index], step * block + t) * rows[t] for t in range(step)]
            held[index] = jnp.where(inside, 0.0, held[index]) - add_tree(pairs)
    return held


pivot_rows = 16


def first_steps(count):
    return count * 3 // 4


def start_inverse(grams, other, scale, after):
    size = grams[0].shape[-1]
    step = pivot_rows
    count = size // step
    own = other is None
    operands = list(grams) + ([] if own else [other])

    def body(*refs):
        parts, refs = refs[: len(grams)], refs[len(grams) :]
        held = []
        for block in range(count):
            at = slice(step * block, step * block + step)
            if own:
                half = size // 2
                here = slice(step * block % half, step * block % half + step)
                core = lax.axis_index("wide") % 2
                total = jnp.where(
                    core == step * block // half, parts[0][here, :], parts[1][here, :]
                )
                refs[3][at, :] = total
                held.append(total * total)
            else:
                total = add_tree([part[at, :] for part in parts])
                held.append(scale * total * refs[0][at, :])
        held_ref, left_ref, right_ref, scale_ref = refs[:3] + refs[4:] if own else refs[1:]
        sub = lax.broadcasted_iota(jnp.int32, (step, size), 0)
        lane = lax.broadcasted_iota(jnp.int32, (step, size), 1)
        diagonals = [
            jnp.where(lane - step * block == sub, held[block], 0.0) for block in range(count)
        ]
        along = lax.rsqrt(jnp.sum(add_tree(diagonals), axis=0, keepdims=True))
        for block in range(count):
            at = slice(step * block, step * block + step)
            down = lax.rsqrt(jnp.sum(diagonals[block], axis=1, keepdims=True))
            held[block] = (held[block] * down) * along
            scale_ref[at, :] = jnp.broadcast_to(down, (step, size)) * along
        held = eliminate(held, left_ref, right_ref, range(first_steps(count)))
        for block in range(count):
            at = slice(step * block, step * block + step)
            held_ref[at, :] = held[block]
            if block >= first_steps(count):
                left_ref[at, :] = jnp.zeros_like(held[block])
                right_ref[at, :] = jnp.zeros_like(held[block])

    outputs = [shaped(size, size)] * (5 if own else 4)
    return kernel_call(body, outputs, operands, about_us=1.8, after=after)


def end_inverse(held, left, right, scaling, after):
    size = held.shape[0]
    step = pivot_rows
    count = size // step

    def body(held_ref, left_in, right_in, scale_ref, out_ref, left_ref, right_ref):
        done = first_steps(count) * step
        left_ref[:done, :] = left_in[:done, :]
        right_ref[:done, :] = right_in[:done, :]
        rows = [held_ref[step * block : step * block + step, :] for block in range(count)]
        eliminate(rows, left_ref, right_ref, range(first_steps(count), count))
        inverse = lax.dot_general(
            left_ref[...],
            right_ref[...],
            (((0,), (0,)), ((), ())),
            precision=precise_level,
            preferred_element_type=jnp.float32,
        )
        out_ref[...] = inverse * scale_ref[...]

    return kernel_call(
        body,
        [shaped(size, size)],
        [held, left, right, scaling],
        scratch=[pltpu.VMEM((size, size), jnp.float32)] * 2,
        about_us=1.6,
        after=after,
    )[0]


def own_part(chip_slice):
    own_blocks, low, rows, rank = chip_slice.shape

    def body(in_ref, out_ref):
        core = lax.axis_index("wide") % low
        for block in range(own_blocks):
            out_ref[block] = in_ref[block, core]

    return kernel_call(body, [shaped(own_blocks, rows, rank)], [chip_slice])[0]


def open_tags(coords, count, rank, after):
    slots, axes = coords.shape

    def body(coords_ref, count_ref, tag_ref, out_ref):
        slot_at = lax.broadcasted_iota(jnp.int32, (slots, 1), 0)
        tag_ref[...] = jnp.zeros_like(tag_ref)
        tag_ref[:slots, :axes] = coords_ref[...].astype(jnp.float32)
        tag_ref[:slots, axes : axes + 1] = (slot_at < count_ref[...]).astype(jnp.float32)
        out_ref[...] = coords_ref[...]

    return kernel_call(
        body,
        [shaped(8, rank), shaped(slots, axes, dtype=jnp.int32)],
        [coords, count],
        after=after,
    )


def stage(value, after):
    def body(in_ref, out_ref, sem):
        copy = pltpu.make_async_copy(in_ref, out_ref, sem)
        copy.start()
        copy.wait()

    return kernel_call(
        body,
        [shaped(*value.shape)],
        [value],
        scratch=[pltpu.SemaphoreType.DMA],
        after=after,
        far=True,
    )[0]


def pack_slices(pairs, single, after):
    own_blocks, low, rows, rank = pairs[0].shape if pairs else (single.shape[0], 0, 0, 0)
    _, rows, rank = single.shape
    total = own_blocks * (low * len(pairs) + 1)

    def body(*refs):
        out_ref = refs[-1]
        for index, ref in enumerate(refs[: len(pairs)]):
            at = index * own_blocks * low
            out_ref[at : at + own_blocks * low] = ref[...].reshape(own_blocks * low, rows, rank)
        out_ref[total - own_blocks :] = refs[len(pairs)][...]

    return kernel_call(
        body, [shaped(total, rows, rank)], list(pairs) + [single], after=after
    )[0]


def gram_of(items):
    rank = items[0].shape[-1]

    def body(*refs):
        rows = jnp.concatenate([ref[...].reshape(-1, rank) for ref in refs[:-1]], axis=0)
        refs[-1][...] = join_gram(gram_parts(rows))

    return kernel_call(body, [shaped(rank, rank)], list(items))[0]


def pick_pieces(coords, own, mine, theirs, gram, narrow_size):
    own_blocks, low, rows, rank = own.shape
    partners, slots, _ = coords.shape
    piece_rows = slots * 2 * low * rows
    share = rank // low

    def body(there_ref, own_ref, mine_ref, theirs_ref, gram_here, *refs):
        out_refs, (coord_ref, gram_ref, all_ref, sem) = refs[:partners], refs[partners:]
        narrow_at = lax.axis_index("narrow")
        core = lax.axis_index("wide") % low
        copy = pltpu.make_async_copy(there_ref, coord_ref, sem)
        copy.start()
        gram_ref[...] = gram_here[...] + join_gram(gram_parts(theirs_ref[...].reshape(-1, rank)))
        for out_ref in out_refs:
            out_ref[piece_rows:, :] = gram_ref[pl.ds(pl.multiple_of(core * share, share), share), :]
        for j in range(low):
            for local in range(own_blocks):
                all_ref[j * own_blocks + local] = own_ref[local, j]
                for m in range(1, narrow_size):
                    last = m == narrow_size - 1
                    holder = j if last else (m - 1) % low
                    at = (m - 1) // low * own_blocks * low + local * low + j
                    if last:
                        at = (narrow_size - 2) * own_blocks + local
                    all_ref[(m * low + j) * own_blocks + local] = jnp.where(
                        core == holder, mine_ref[at], theirs_ref[at]
                    )
        copy.wait()
        for d, out_ref in enumerate(out_refs):
            for pair in range(slots * 2):
                block = coord_ref[d, pair // 2, 1 + pair % 2]
                owner = (block // own_blocks) ^ narrow_at
                for j in range(low):
                    at = (owner * low + (core ^ j)) * own_blocks + block % own_blocks
                    to = (pair * low + j) * rows
                    out_ref[to : to + rows, :] = all_ref[at]

    return kernel_call(
        body,
        [shaped(piece_rows + share, rank)] * partners,
        [coords, own, mine, theirs, gram],
        scratch=[
            pltpu.SMEM(coords.shape, jnp.int32),
            pltpu.VMEM((rank, rank), jnp.float32),
            pltpu.VMEM((narrow_size * low * own_blocks, rows, rank), jnp.float32),
            pltpu.SemaphoreType.DMA,
        ],
    )


def first_mode(tags, pieces, spread, wide_size, low, after):
    rank = pieces[0].shape[1]
    slots, _, width = spread.shape
    edge = width // 4
    pairs = 2 * slots
    slice_rows = edge // wide_size
    chunk = 4

    def body(tag_ref, *refs):
        piece_refs = refs[: len(pieces)]
        spread_ref, rows_ref, term_ref, held_ref = refs[len(pieces) :]
        term_ref[slots * edge :, :] = tag_ref[...]
        wide_at = lax.axis_index("wide")
        for d, piece_ref in enumerate(piece_refs):
            for j in range(low):
                place = wide_at ^ (d * low + j)
                for pair in range(pairs):
                    at = (pair * low + j) * slice_rows
                    held_ref[pair, place] = piece_ref[at : at + slice_rows, :]
        rows_ref[...] = held_ref[...].reshape(pairs, edge, rank)
        for slot in range(slots):
            stacked = stack_parts(rows_ref[2 * slot + 1])

            def step(index, total):
                at = pl.multiple_of(index * (chunk * edge), chunk * edge)
                product = dot32(spread_ref[slot, pl.ds(at, chunk * edge), :], stacked)
                product = product[:, :rank] + product[:, rank:]
                for inner in range(chunk):
                    row = rows_ref[2 * slot, pl.ds(index * chunk + inner, 1), :]
                    total = total + product[inner * edge : (inner + 1) * edge] * row
                return total

            total = lax.fori_loop(
                0, edge // chunk, step, jnp.zeros((edge, rank), jnp.float32), unroll=True
            )
            live = tag_ref[slot : slot + 1, live_at : live_at + 1]
            term_ref[slot * edge : (slot + 1) * edge, :] = total * live

    return kernel_call(
        body,
        [shaped(pairs, edge, rank), shaped(slots * edge + tags.shape[0], rank)],
        [tags] + list(pieces) + [spread],
        scratch=[pltpu.VMEM((pairs, wide_size, slice_rows, rank), jnp.float32)],
        about_us=3.0,
        after=after,
    )


def split_blocks(blocks, after):
    slots, edge, pairs = blocks.shape
    turn = 512
    lanes = 2 * edge

    def body(in_ref, spread_ref, turned_ref):
        left = lax.broadcasted_iota(jnp.int32, (edge, lanes), 1) < edge

        def roll(value):
            return pltpu.roll(value, edge, 1)

        for slot in range(slots):

            @pl.loop(0, pairs // turn)
            def _(index):
                at = pl.multiple_of(index * turn, turn)
                parts = []
                for inner in range(turn // lanes):
                    value = in_ref[slot, :, pl.ds(at + inner * lanes, lanes)]
                    high = value.astype(jnp.bfloat16).astype(jnp.float32)
                    rest = value - high
                    middle = rest.astype(jnp.bfloat16).astype(jnp.float32)
                    low = rest - middle
                    first = roll(jnp.where(left, middle, high))
                    second = roll(jnp.where(left, high, low))
                    rows = [
                        [jnp.where(left, high, first), jnp.where(left, low, second)],
                        [jnp.where(left, first, middle), jnp.where(left, second, high)],
                    ]
                    row_at = pl.multiple_of((at // lanes + inner) * lanes, lanes)
                    for half in range(2):
                        spread_ref[slot, pl.ds(row_at + half * edge, edge), :] = jnp.concatenate(
                            rows[half], axis=1
                        ).astype(jnp.bfloat16)
                    parts.append([item.astype(jnp.bfloat16) for item in (high, middle, low)])
                high, middle, low = [jnp.concatenate(item, axis=1) for item in zip(*parts)]
                here = pl.ds(at, turn)
                turned_ref[slot, here, : 2 * edge] = jnp.concatenate([high, middle], axis=0).T
                turned_ref[slot, here, 2 * edge :] = jnp.concatenate([low, high], axis=0).T

    kind = shaped(slots, pairs, 4 * edge, dtype=jnp.bfloat16)
    return kernel_call(body, [kind, kind], [blocks], after=after)


def dot32(left, right):
    return jnp.dot(left, right, preferred_element_type=jnp.float32)


def times(rows, matrix):
    rank = matrix.shape[1]
    high, middle, least = split3(matrix)
    left_high, left_middle, left_least = split3(rows)
    one = jnp.concatenate([high, middle], axis=1)
    wide = dot32(
        jnp.concatenate([left_high, left_middle], axis=1), jnp.concatenate([one, one], axis=0)
    )
    thin = dot32(
        jnp.concatenate([left_least, left_high], axis=1), jnp.concatenate([high, least], axis=0)
    )
    return (thin + wide[:, rank:]) + wide[:, :rank]


def stack_parts(matrix):
    high, middle, least = split3(matrix)
    none = jnp.zeros_like(high)
    return jnp.concatenate(
        [
            jnp.concatenate([high, high, high, none], axis=0),
            jnp.concatenate([middle, middle, none, least], axis=0),
        ],
        axis=1,
    )


def gram_parts(rows):
    rank = rows.shape[1]
    high, middle, least = split3(rows)
    both = jnp.concatenate([high, middle], axis=1)
    turned = both.T
    return dot32(turned, both), dot32(turned[:rank], least)


def join_gram(parts):
    square, rest = parts
    rank = rest.shape[0]
    rest = rest + square[:rank, rank:]
    return (square[rank:, rank:] + (rest + rest.T)) + square[:rank, :rank]


def split3(value):
    high = value.astype(jnp.bfloat16)
    rest = value - high.astype(jnp.float32)
    middle = rest.astype(jnp.bfloat16)
    low = (rest - middle.astype(jnp.float32)).astype(jnp.bfloat16)
    return high, middle, low


def tag_of(ref, d, slots, edge, slot, at):
    return ref[d, slots * edge + slot : slots * edge + slot + 1, at : at + 1]


def sum_terms(terms, own, slots, edge, after):
    partners, _, rank = terms.shape

    def body(term_ref, own_ref, out_ref):
        for slot in range(slots):
            here = tag_of(own_ref, 0, slots, edge, slot, 0)
            total = None
            for d in range(partners):
                for other in range(slots):
                    same = (tag_of(term_ref, d, slots, edge, other, 0) == here).astype(jnp.float32)
                    part = term_ref[d, other * edge : (other + 1) * edge, :] * same
                    total = part if total is None else total + part
            out_ref[slot * edge : (slot + 1) * edge, :] = total

    return kernel_call(body, [shaped(slots * edge, rank)], [terms, own], after=after)[0]


def second_mode(partial, terms, inverse, spread_blocks, rows, wide_size):
    low = len(terms)
    pairs, edge, rank = rows.shape
    slots = pairs // 2
    slice_rows = edge // wide_size
    chunk = 4

    def body(partial_ref, *refs):
        term_refs = refs[: len(terms)]
        inverse_ref, spread_ref, rows_ref = refs[len(terms) : len(terms) + 3]
        out_refs = refs[len(terms) + 3 : len(terms) + 3 + low]
        held_ref = refs[-1]
        sums = []
        for slot in range(slots):
            total = partial_ref[slot * edge : (slot + 1) * edge, :]
            here = tag_of(term_refs[0], 0, slots, edge, slot, 0)
            for m in range(wide_size):
                if m % low == 0:
                    continue
                for other in range(slots):
                    there = tag_of(term_refs[m % low], m // low, slots, edge, other, 0)
                    same = (there == here).astype(jnp.float32)
                    part = term_refs[m % low][m // low, other * edge : (other + 1) * edge, :]
                    total = total + part * same
            sums.append(total)
        aux = times(jnp.concatenate(sums, axis=0), inverse_ref[...])
        for slot in range(slots):
            weight = tag_of(term_refs[0], 0, slots, edge, slot, live_at)
            stacked = stack_parts(aux[slot * edge : (slot + 1) * edge] * weight)
            rows_i, rows_j = rows_ref[2 * slot], rows_ref[2 * slot + 1]

            def step(index, total_j):
                at = pl.multiple_of(index * (chunk * edge), chunk * edge)
                spread = jnp.dot(
                    spread_ref[slot, pl.ds(at, chunk * edge), :],
                    stacked,
                    preferred_element_type=jnp.float32,
                )
                spread = spread[:, :rank] + spread[:, rank:]
                for inner in range(chunk):
                    part = spread[inner * edge : (inner + 1) * edge]
                    here = index * chunk + inner
                    held_ref[2 * slot, pl.ds(here, 1), :] = jnp.sum(
                        part * rows_j, axis=0, keepdims=True
                    )
                    total_j = total_j + part * rows_ref[2 * slot, pl.ds(here, 1), :]
                return total_j

            held_ref[2 * slot + 1] = lax.fori_loop(
                0, edge // chunk, step, jnp.zeros((edge, rank), jnp.float32), unroll=True
            )
        wide_at = lax.axis_index("wide")
        for place in range(wide_size):
            source = (wide_at ^ place) * slice_rows
            for pair in range(2 * slots):
                out_refs[place % low][place // low, pair] = held_ref[
                    pair, pl.ds(pl.multiple_of(source, slice_rows), slice_rows), :
                ]

    return kernel_call(
        body,
        [shaped(wide_size // low, 2 * slots, slice_rows, rank)] * low,
        [partial] + list(terms) + [inverse, spread_blocks, rows],
        scratch=[pltpu.VMEM((2 * slots, edge, rank), jnp.float32)],
        about_us=2.5,
    )


def read_coords(terms, slots, edge, axes):
    low = len(terms)
    partners = terms[0].shape[0]

    def body(*refs):
        for j in range(low):
            for d in range(partners):
                tags = refs[j][d, slots * edge : slots * (edge + 1), :axes]
                refs[-1][d * low + j] = tags.astype(jnp.int32)

    return kernel_call(
        body, [shaped(partners * low, slots, axes, dtype=jnp.int32)], list(terms)
    )[0]


def column_gram(coords, terms, inverse, edge, after):
    low = len(terms)
    devices, slots, _ = coords.shape
    rank = inverse.shape[0]
    count = devices * slots

    def body(coord_ref, *refs):
        term_refs = refs[:low]
        inverse_ref, gram_ref, aux_ref = refs[low:]
        wide_at = lax.axis_index("wide")
        aux_ref[...] = jnp.zeros_like(aux_ref)
        blocks_at = [
            coord_ref[wide_at ^ (index // slots), index % slots, 0] for index in range(count)
        ]
        for index in range(count):
            to = jnp.int32(index)
            for earlier in reversed(range(index)):
                to = jnp.where(blocks_at[earlier] == blocks_at[index], earlier, to)
            here = slice(index % slots * edge, (index % slots + 1) * edge)
            place = wide_at ^ (index // slots)
            term = term_refs[0][place // low, here, :]
            for j in range(1, low):
                term = jnp.where(place % low == j, term_refs[j][place // low, here, :], term)
            aux_ref[to] += term
        aux = times(aux_ref[...].reshape(count * edge, rank), inverse_ref[...])
        aux_ref[...] = aux.reshape(count, edge, rank)
        gram_ref[...] = join_gram(gram_parts(aux))

    return kernel_call(
        body,
        [shaped(rank, rank), shaped(count, edge, rank)],
        [coords] + list(terms) + [inverse],
        scalars=1,
        about_us=0.1,
        after=after,
    )


def own_aux(coords, aux, own_rows, after):
    devices, slots, _ = coords.shape
    count, edge, rank = aux.shape
    grain = min(own_rows, edge)
    per_block = edge // grain
    per_device = own_rows // grain

    def body(coord_ref, aux_ref, out_ref, done_ref):
        done_ref[...] = jnp.zeros_like(done_ref)
        out_ref[...] = jnp.zeros_like(out_ref)
        wide_at = lax.axis_index("wide")
        blocks_at = [
            coord_ref[wide_at ^ (index // slots), index % slots, 0] for index in range(count)
        ]
        for index in range(count):
            first = jnp.bool_(True)
            for earlier in range(index):
                first = first & (blocks_at[earlier] != blocks_at[index])
            for part in range(per_block):
                grain_at = blocks_at[index] * per_block + part

                @pl.when(first & (grain_at // per_device == wide_at))
                def _():
                    out_ref[grain_at % per_device] = aux_ref[
                        index, part * grain : (part + 1) * grain, :
                    ]

    owned, done = kernel_call(
        body,
        [shaped(per_device, grain, rank), shaped(8, rank)],
        [coords, aux],
        scalars=1,
        about_us=0.1,
        after=after,
    )
    return owned.reshape(own_rows, rank), done


def pack_pieces(groups, after):
    low = len(groups)
    partners = groups[0].shape[0]

    def body(*refs):
        for d in range(partners):
            for j in range(low):
                refs[low + d][j] = refs[j][d]

    return kernel_call(
        body, [shaped(low, *groups[0].shape[1:])] * partners, list(groups), after=after
    )


def pack_whole(items, after=(), rows=None):
    rows = rows or items[0].shape[0]
    kind = shaped(len(items), rows, *items[0].shape[1:], dtype=items[0].dtype)

    def body(*refs):
        for index, ref in enumerate(refs[:-1]):
            refs[-1][index] = ref[:rows]

    return kernel_call(body, [kind], list(items), after=after)[0]


def with_partners(value, low):
    return [value] + [swap_with(value, "wide", j) for j in range(1, low)]


def plan_sums(coords, rows, narrow_size, own_blocks, after):
    devices, slots, _ = coords.shape
    count = devices * slots * 2
    lanes = min(count * rows, 128)

    def body(coord_ref, out_ref, held_ref):
        narrow_at = lax.axis_index("narrow")
        held_ref[...] = jnp.zeros_like(held_ref)
        ahead = lax.broadcasted_iota(jnp.int32, (rows, lanes), 1) - lax.broadcasted_iota(
            jnp.int32, (rows, lanes), 0
        )
        for index in range(count):
            pair = index % (2 * slots)
            block = coord_ref[index // (2 * slots), pair // 2, 1 + pair % 2]
            to = ((block // own_blocks) ^ narrow_at) * own_blocks + block % own_blocks
            at = index * rows // lanes * lanes
            held_ref[to, :, at : at + lanes] += (ahead == index * rows - at).astype(jnp.float32)
        out_ref[...] = held_ref[...].reshape(out_ref.shape).astype(jnp.bfloat16)

    total = narrow_size * own_blocks
    return kernel_call(
        body,
        [shaped(total * rows, count * rows, dtype=jnp.bfloat16)],
        [coords],
        scalars=1,
        scratch=[pltpu.VMEM((total, rows, count * rows), jnp.float32)],
        after=after,
    )[0]


def add_pieces(plan, pieces, narrow_size, after):
    low, pairs, rows, rank = pieces[0].shape
    part_rows = plan.shape[0] // narrow_size

    def body(plan_ref, *refs):
        terms = jnp.concatenate(
            [ref[...].reshape(low * pairs * rows, rank) for ref in refs[: len(pieces)]], axis=0
        )
        high, middle, least = split3(terms)
        wide = dot32(plan_ref[...], jnp.concatenate([high, middle], axis=1))
        sums = (dot32(plan_ref[...], least) + wide[:, rank:]) + wide[:, :rank]
        for m, out_ref in enumerate(refs[len(pieces) :]):
            out_ref[...] = sums[m * part_rows : (m + 1) * part_rows]

    return kernel_call(
        body, [shaped(part_rows, rank)] * narrow_size, [plan] + list(pieces), after=after
    )


def add_parts(parts, after=(), rows=None):
    count, rank = parts[0].shape
    rows = rows or count

    def body(*refs):
        refs[-1][...] = add_tree([ref[count - rows :, :] for ref in refs[:-1]])

    return kernel_call(body, [shaped(rows, rank)], list(parts), after=after)[0]


def solve_rows(rows, inverse, after):
    shape = rows.shape

    def body(rows_ref, inverse_ref, out_ref):
        solved = times(rows_ref[...].reshape(-1, shape[-1]), inverse_ref[...])
        out_ref[...] = solved.reshape(shape)

    return kernel_call(body, [shaped(*shape)], [rows, inverse], after=after)[0]


def lay_rows(solved, others, inverse, own_blocks):
    low = 1 + len(others)
    partners, part_rows, rank = solved.shape
    rows = part_rows // own_blocks

    def body(solved_ref, *refs):
        wide_at = lax.axis_index("wide")
        inverse_ref, out_ref = refs[len(others) :]
        for j in range(low):
            if j == 0:
                value = solved_ref[...].reshape(partners * part_rows, rank)
            else:
                value = times(
                    refs[j - 1][...].reshape(partners * part_rows, rank), inverse_ref[...]
                )
            for d in range(partners):
                place = wide_at ^ (d * low + j)
                for block in range(own_blocks):
                    at = d * part_rows + block * rows
                    out_ref[block, place] = value[at : at + rows]

    return kernel_call(
        body,
        [shaped(own_blocks, partners * low, rows, rank)],
        [solved] + list(others) + [inverse],
    )[0]


def on_device(blocks, block_coords, block_count, orbital_factor):
    slots, edge = blocks.shape[2:4]
    rank = orbital_factor.shape[1]
    wide_size = lax.axis_size("wide")
    narrow_size = lax.axis_size("narrow")
    low = digits_of(wide_size)[0][1]
    slice_rows = edge // wide_size
    own_blocks = orbital_factor.shape[0] // edge
    own_rows = NP // narrow_size // wide_size

    by_slice = orbital_factor.reshape(own_blocks, wide_size // low, low, slice_rows, rank)
    chip_at = lax.axis_index("wide") // low
    chip_slice = lax.dynamic_index_in_dim(by_slice, chip_at, 1, keepdims=False)
    own_slice = own_part(chip_slice)
    pairs = [send_by_core(chip_slice, [m, m + 1]) for m in range(1, narrow_size - 1, low)]
    single = swap_with(own_slice, "narrow", narrow_size - 1)
    arrived = gather_from(block_coords[0, 0], "wide", skip=1)[1:]
    blocks = stage(blocks[0, 0], [own_slice])
    mine = pack_slices(pairs, single, arrived + [blocks])
    theirs = swap_with(mine, "wide", 1)
    tags, coords = open_tags(block_coords[0, 0], block_count, rank, [mine])
    coords = pack_whole([coords] + arrived)
    gram = gram_of([chip_slice, mine])
    wanted = pick_pieces(coords, chip_slice, mine, theirs, gram, narrow_size)
    pieces = exchange(wanted, "wide", skip=1)

    spread, turned = split_blocks(blocks, wanted[:1])
    half = add_parts(pieces, [turned], rows=rank // low)
    rows, terms = first_mode(tags, pieces, spread, wide_size, low, [half])
    other_half = swap_with(half, "wide", 1)
    terms = add_parts([terms], [other_half])
    held, left, right, gram_b, scaling = start_inverse([half, other_half], None, 1.0, [terms])
    started = [held, left, right, scaling]
    terms = pack_whole(gather_from(terms, "wide", skip=1), after=started[:1])
    inverse_b = end_inverse(*started, [terms])
    column_terms = with_partners(terms, low)
    all_coords = read_coords(column_terms, slots, edge, block_coords.shape[3])

    partial = sum_terms(terms, terms, slots, edge, [inverse_b])
    groups = second_mode(partial, column_terms, inverse_b, turned, rows, wide_size)
    plan = plan_sums(all_coords, slice_rows, narrow_size, own_blocks, groups[:1])
    groups = [groups[0]] + [swap_with(groups[j], "wide", j) for j in range(1, low)]
    packed = pack_pieces(groups, [plan])
    pieces = exchange(packed, "wide", skip=1)

    gram, aux = column_gram(all_coords, column_terms, inverse_b, edge, packed[:1])

    sums = add_pieces(plan, pieces, narrow_size, [gram])
    parts = exchange(sums, "narrow")
    step = narrow_size // 2
    while step > 1:
        gram = add_parts([gram, swap_with(gram, "narrow", step)], sums[:1])
        step //= 2
    aux_owned, done = own_aux(all_coords, aux, own_rows, [gram])
    total = add_parts(parts, [gram, done])
    grams = [gram, swap_with(gram, "narrow", step)]
    started = start_inverse(grams, gram_b, 2.0, [total])
    totals = pack_whole(gather_from(total, "wide", skip=1), after=started[:1])
    inverse_a = end_inverse(*started, [totals])
    solved = solve_rows(totals, inverse_a, [])
    orbital_new = lay_rows(solved, with_partners(totals, low)[1:], inverse_a, own_blocks)
    return (aux_owned[None], orbital_new.reshape(own_blocks * edge, rank))


def solution(mesh):
    return jax.shard_map(
        on_device,
        mesh=mesh,
        in_specs=(
            P("wide", "narrow", None, None, None),
            P("wide", "narrow", None, None),
            P("wide", "narrow"),
            P("narrow", None),
        ),
        out_specs=(P("narrow", "wide", None), P("narrow", None)),
        check_vma=False,
    )
```
